32 devices in a mesh: cells: 8 (over z, x), vecs: 4 (over y, core).
Axes of the slice: x: 2, y: 2, z: 4, core: 2. Of those that a mesh axis runs over, the one named last changes fastest.
Arguments:
- wave_block: float32 [64, 73728], P('vecs', 'cells'), may hold values from -6 to 6
- connectivity: int32 [125, 1024], P(None, 'cells'), may hold values from 0 to 10304, as said below
- send_list: int32 [8712], P('cells'), may hold values from 0 to 9215, as said below
- levels: int32 [1024], P('cells'), may hold values from 0 to 2
- live_cells: int32 [8], P('cells'), may hold values from 64 to 128, as said below
- potential: float32 [125, 1024], P(None, 'cells'), may hold values from -24 to 8
- mass_scale: float32 [73728], P('cells'), may hold values from 0.5 to 2
- center: float32 [], replicated, may hold values from 20 to 30
- halfwidth: float32 [], replicated, may hold values from 25 to 35
- earlier_vectors: bfloat16 [2048, 73728], P(None, ('cells', 'vecs')), may hold values from -0.0234375 to 0.0234375
Outputs:
- filtered: float32 [64, 73728], P(None, ('cells', 'vecs'))
- projections: float32 [2048, 64], P(('cells', 'vecs'))
The draws below stay inside these ranges and needn't reach their ends.
Inputs may be any that keep to these rules, and one draw needn't show every extreme that they name: `connectivity`: column c names the slots of cell c's 125 nodes on its device, node (a,b,c) of the reference cube at row 25 a + 5 b + c. A device's cells form a structured block of 8 x 8 x 2 cells of degree 4 in Morton order, nodes numbered at random over the 9216 node slots; the face of the block toward the device before it lies in the ghost slots 9216 to 10304 in the order of that device's send_list, so that exactly 64 cells of each device name ghost slots. `send_list`: A device's 1089 entries are distinct node slots of its block's face toward the device after it. Cells 0 to live_cells - 1 of a device are in use, the rest of its slots are empty; some device uses all 128, some only 64.
All inputs are finite; a program needn't handle non-finite values.
Results may differ from the reference program's by a relative error of at most 0.0031.
Values may be sent and summed in bfloat16 or wider, within the bound.
A program may use at most 128 MiB of HBM per device.

```python
import math
import jax
import jax.numpy as jnp
import numpy as np
from jax import lax

NVEC = 64
PREV = 2048
FXY = 8
LZ = 2
CELL_DEV = 128
GHOST = 1089
OWN = 9216
CELLS = 1024
NODES = 73728
N_CELLS = 8


def number_device(device_key):
    return jax.random.permutation(device_key, OWN).astype(jnp.int32)


def mesh_tables(key):
    side_nodes = 4 * FXY + 1
    face_nodes = side_nodes * side_nodes
    layer_nodes = 4 * LZ
    grid_x, grid_y, grid_z = np.meshgrid(np.arange(FXY), np.arange(FXY), np.arange(LZ), indexing='ij')
    grid_x = grid_x.reshape(-1)
    grid_y = grid_y.reshape(-1)
    grid_z = grid_z.reshape(-1)
    morton_codes = np.zeros(grid_x.shape, dtype=grid_x.dtype)
    for bit_index in range(8):
        morton_codes = morton_codes | (grid_x >> bit_index & 1) << 3 * bit_index | (grid_y >> bit_index & 1) << 3 * bit_index + 1 | (grid_z >> bit_index & 1) << 3 * bit_index + 2
    morton_rank = np.argsort(morton_codes, kind='stable')
    local_a, local_b, local_c = np.meshgrid(np.arange(5), np.arange(5), np.arange(5), indexing='ij')
    local_a = local_a.reshape(-1)
    local_b = local_b.reshape(-1)
    local_c = local_c.reshape(-1)
    node_x = 4 * grid_x[morton_rank][None, :] + local_a[:, None]
    node_y = 4 * grid_y[morton_rank][None, :] + local_b[:, None]
    node_z = 4 * grid_z[morton_rank][None, :] + local_c[:, None]
    planar = node_x * side_nodes + node_y
    structured = np.where(node_z == 0, OWN + planar, (node_z - 1) * face_nodes + planar)
    device_keys = jax.random.split(jax.random.fold_in(key, 11), N_CELLS)
    numbering = jax.vmap(number_device)(device_keys)
    table = jnp.asarray(structured, jnp.int32)
    relabelled = jnp.where(table[None] >= OWN, table[None], numbering[:, jnp.minimum(table, OWN - 1)])
    top_face = numbering[:, (layer_nodes - 1) * face_nodes + jnp.arange(face_nodes, dtype=jnp.int32)]
    return (relabelled.astype(jnp.int32), top_face.astype(jnp.int32))


def draw_connectivity(key, part):
    relabelled, top_face = mesh_tables(key)
    return relabelled.transpose(1, 0, 2).reshape(125, CELLS)


def draw_send_list(key, part):
    relabelled, top_face = mesh_tables(key)
    return top_face.reshape(GHOST * N_CELLS)


def draw_live_cells(key, part):
    counts_drawn = jax.random.randint(jax.random.fold_in(key, 3), (N_CELLS,), CELL_DEV // 2, CELL_DEV + 1)
    device_rank = jax.random.permutation(jax.random.fold_in(key, 5), N_CELLS)
    counts_drawn = counts_drawn.at[device_rank[0]].set(CELL_DEV)
    counts_drawn = counts_drawn.at[device_rank[1]].set(CELL_DEV // 2)
    return counts_drawn.astype(jnp.int32)


def touch_ends(result, key, least, largest):
    spot = [jax.random.randint(jax.random.fold_in(key, axis), (), 0, length) for axis, length in enumerate(result.shape)]
    longest = result.shape.index(max(result.shape))
    next_to = spot[:longest] + [(spot[longest] + 1) % result.shape[longest]] + spot[longest + 1:]
    return result.at[tuple(spot)].set(least).at[tuple(next_to)].set(largest)


def level_of(stream_key, shape, cuts, smallest, top_value):
    def one(axis_at, shards_of):
        heights = jax.random.uniform(jax.random.fold_in(jax.random.fold_in(stream_key, 6), axis_at), (shards_of,), jnp.float32, smallest / len(cuts), top_value / len(cuts))
        return jnp.repeat(jnp.exp(heights), shape[axis_at] // shards_of).reshape((-1,) + (1,) * (len(shape) - axis_at - 1))

    gain = one(*cuts[0])
    for cut in cuts[1:]:
        gain = gain * one(*cut)
    return gain


def gaussian(own_key, shape, spread, most, cuts=(), kind=jnp.bfloat16):
    values = jax.random.normal(own_key, shape, jnp.float32) * spread
    if len(cuts) > 0:
        values = level_of(own_key, shape, cuts, -0.22, 0.18) * values
    return jnp.clip(values, min=-most, max=most).astype(kind)


def setup_inputs(seed: int = 0) -> dict:
    splits = jax.random.split(jax.random.key(seed), 11)
    return {
        "wave_block": gaussian(splits[0], (NVEC, NODES), 1.0, 6.0, ((0, 4), (1, 8)), jnp.float32),
        "connectivity": draw_connectivity(jax.random.fold_in(splits[10], 71), 0),
        "send_list": draw_send_list(jax.random.fold_in(splits[10], 71), 0),
        "levels": touch_ends(jax.random.randint(splits[3], (CELLS,), 0, 3), jax.random.fold_in(splits[3], 1), 0, 2).astype(jnp.int32),
        "live_cells": draw_live_cells(jax.random.fold_in(splits[10], 71), 0),
        "potential": jnp.clip(-24.0 + 32.0 * jax.random.uniform(splits[5], (125, CELLS), jnp.float32) ** level_of(splits[5], (125, CELLS), ((1, 8),), -0.2, 0.2), -24.0, 8.0),
        "mass_scale": jnp.clip(jnp.exp(math.log(2.0) - 1.3862944 * jax.random.uniform(splits[6], (NODES,), jnp.float32) ** level_of(splits[6], (NODES,), ((0, 8),), -0.2, 0.2)), 0.5, 2.0),
        "center": jnp.clip(jax.random.uniform(splits[7], (), jnp.float32, 20.0, 30.0), 20.0, 30.0),
        "halfwidth": jnp.clip(jax.random.uniform(splits[8], (), jnp.float32, 25.0, 35.0), 25.0, 35.0),
        "earlier_vectors": gaussian(splits[9], (PREV, NODES), NODES ** -0.5, 0.0234375, ((1, 32),)),
    }


def gll_tables():
    root_value = math.sqrt(3.0 / 7.0)
    points = np.array([-1.0, -root_value, 0.0, root_value, 1.0])
    weights = np.array([0.1, 49.0 / 90.0, 32.0 / 45.0, 49.0 / 90.0, 0.1])
    barycentric = np.ones(5)
    for node_index in range(5):
        for other_node in range(5):
            if other_node != node_index:
                barycentric[node_index] = barycentric[node_index] / (points[node_index] - points[other_node])
    derivative = np.zeros((5, 5))
    for row_index in range(5):
        for col_index in range(5):
            if row_index != col_index:
                derivative[row_index, col_index] = barycentric[col_index] / barycentric[row_index] / (points[row_index] - points[col_index])
        derivative[row_index, row_index] = -np.sum(derivative[row_index])
    mass_one = np.zeros((5, 5))
    for node_index in range(5):
        mass_one[node_index, node_index] = weights[node_index]
    laplace_one = derivative.T @ mass_one @ derivative
    stiffness = np.kron(np.kron(laplace_one, mass_one), mass_one) + np.kron(np.kron(mass_one, laplace_one), mass_one) + np.kron(np.kron(mass_one, mass_one), laplace_one)
    quadrature = np.kron(np.kron(weights, weights), weights)
    return (stiffness.astype(np.float32), quadrature.astype(np.float32))

def reference(wave_block, connectivity, send_list, levels, live_cells, potential, mass_scale, center, halfwidth, earlier_vectors):
    stiffness, quadrature = gll_tables()
    stiffness_low = jnp.asarray(stiffness).astype(jnp.bfloat16)
    quad_weights = jnp.asarray(quadrature).astype(jnp.float32)
    conn_dev = connectivity.reshape(125, N_CELLS, CELL_DEV).transpose(1, 0, 2)
    pot_dev = potential.reshape(125, N_CELLS, CELL_DEV).transpose(1, 0, 2)
    send_dev = send_list.reshape(N_CELLS, GHOST)
    cell_size = jnp.exp2(-levels.astype(jnp.float32)).reshape(N_CELLS, CELL_DEV)
    in_use = (jnp.arange(CELL_DEV, dtype=jnp.int32)[None, :] < live_cells[:, None]).astype(jnp.float32)
    kinetic = cell_size / 4.0 * in_use
    volume = cell_size ** 3 / 8.0 * in_use
    coefficient = volume[:, None, :] * quad_weights[None, :, None] * pot_dev

    def cell_sum(inputs):
        extended, cells_conn, kin_part, coeff_part = inputs
        values = extended[:, cells_conn].astype(jnp.bfloat16)
        stiff_part = jnp.einsum('jk,vkc->vjc', stiffness_low.astype(jnp.float32), values.astype(jnp.float32))
        cell_terms = kin_part[None, None, :] * stiff_part + coeff_part[None] * values.astype(jnp.float32)
        return jnp.zeros((NVEC, OWN + GHOST), jnp.float32).at[:, cells_conn].add(cell_terms)

    def take_face(vectors, slots):
        return vectors[:, slots]

    def add_back(sums, returned, slots):
        return sums[:, :OWN].at[:, slots].add(returned)

    def apply_operator(vectors):
        scaled = vectors * mass_scale[None, :]
        per_dev = scaled.reshape(NVEC, N_CELLS, OWN).transpose(1, 0, 2)
        top_faces = jax.vmap(take_face)(per_dev, send_dev)
        ghosts = jnp.concatenate([jnp.zeros((1, NVEC, GHOST), jnp.float32), top_faces[:-1]], 0)
        extended = jnp.concatenate([per_dev, ghosts], 2)
        slot_sums = lax.map(cell_sum, (extended, conn_dev, kinetic, coefficient))
        returned = jnp.concatenate([slot_sums[1:, :, OWN:], jnp.zeros((1, NVEC, GHOST), jnp.float32)], 0)
        owned = jax.vmap(add_back)(slot_sums, returned, send_dev)
        return owned.transpose(1, 0, 2).reshape(NVEC, NODES) * mass_scale[None, :]
    degree_one = (apply_operator(wave_block) - center * wave_block) / halfwidth
    degree_two = 2.0 * (apply_operator(degree_one) - center * degree_one) / halfwidth - wave_block
    rounded = degree_two.astype(jnp.bfloat16)
    projections = jnp.dot(earlier_vectors, rounded.T, preferred_element_type=jnp.float32)
    projection_low = projections.astype(jnp.bfloat16)
    filtered = rounded.astype(jnp.float32) - jnp.dot(projection_low.T, earlier_vectors, preferred_element_type=jnp.float32)
    return (filtered, projections)
```

```python
import functools
import math

import jax
import jax.numpy as jnp
import numpy as np
from jax import lax
from jax.experimental import pallas as pl
from jax.experimental.pallas import tpu as pltpu
from jax.sharding import PartitionSpec as P

ROWS = 200
HALF = 63
VMEM_BYTES = 48 * 1024 * 1024


def passed_along(value, axis, steps):
    count = lax.axis_size(axis)
    leading, last = (max(0, -steps), min(count, count - steps))
    return lax.ppermute(value, axis, [(source, source + steps) for source in range(leading, last)])


def gll_tables():
    root_value = math.sqrt(3.0 / 7.0)
    points = np.array([-1.0, -root_value, 0.0, root_value, 1.0])
    weights = np.array([0.1, 49.0 / 90.0, 32.0 / 45.0, 49.0 / 90.0, 0.1])
    barycentric = np.ones(5)
    for node_index in range(5):
        for other_node in range(5):
            if other_node != node_index:
                barycentric[node_index] = barycentric[node_index] / (
                    points[node_index] - points[other_node]
                )
    derivative = np.zeros((5, 5))
    for row_index in range(5):
        for col_index in range(5):
            if row_index != col_index:
                derivative[row_index, col_index] = (
                    barycentric[col_index]
                    / barycentric[row_index]
                    / (points[row_index] - points[col_index])
                )
        derivative[row_index, row_index] = -np.sum(derivative[row_index])
    mass_one = np.zeros((5, 5))
    for node_index in range(5):
        mass_one[node_index, node_index] = weights[node_index]
    laplace_one = derivative.T @ mass_one @ derivative
    stiffness = (
        np.kron(np.kron(laplace_one, mass_one), mass_one)
        + np.kron(np.kron(mass_one, laplace_one), mass_one)
        + np.kron(np.kron(mass_one, mass_one), laplace_one)
    )
    quadrature = np.kron(np.kron(weights, weights), weights)
    return (stiffness.astype(np.float32), quadrature.astype(np.float32))


def fixed_tables():
    stiffness, quadrature = gll_tables()
    spread = np.zeros((208, 128), np.float32)
    for j in range(125):
        spread[8 * (j // 5) + j % 5, j] = 1.0
    spread[200, 125] = 1.0
    padded = spread[:200, :125] @ stiffness @ spread[:200, :125].T
    reorder = np.zeros((128, 128), np.float32)
    for rank in range(128):
        bit = [rank >> k & 1 for k in range(7)]
        x = bit[0] + 2 * bit[3] + 4 * bit[5]
        y = bit[1] + 2 * bit[4] + 4 * bit[6]
        reorder[rank, 64 * bit[2] + 8 * x + y] = 1.0
    return padded, quadrature, spread, reorder


def lane_iota(shape):
    return lax.broadcasted_iota(jnp.int32, shape, 1)


def row_iota(shape):
    return lax.broadcasted_iota(jnp.int32, shape, 0)


def gather_kernel(
    wave, mass, conn_high, conn_low, cell_data, spread, reorder,
    nodal, face, inverse, cell_out, packed, low, high, stage,
):
    chunks = wave.shape[1] // 256
    vectors = wave.shape[0]
    group = vectors + 8
    order = reorder[...]
    order_low = order.astype(jnp.bfloat16)
    high[...] = jnp.dot(conn_high[...], order_low, preferred_element_type=jnp.float32).astype(jnp.int32)
    low[...] = jnp.dot(conn_low[...], order_low, preferred_element_type=jnp.float32).astype(jnp.int32)
    exact = lax.Precision.HIGHEST
    ordered = jnp.dot(cell_data[...], order, precision=exact, preferred_element_type=jnp.float32)
    cell_out[...] = jnp.dot(spread[...], ordered, precision=exact, preferred_element_type=jnp.float32)
    for chunk in range(chunks):
        columns = slice(256 * chunk, 256 * chunk + 256)
        scale = mass[:, columns]
        packed[group * chunk:group * chunk + vectors, :] = wave[:, columns] * scale
        packed[group * chunk + vectors:group * chunk + group, :] = jnp.broadcast_to(scale, (8, 256))
    value = packed[...]
    value_high = value.astype(jnp.bfloat16)
    value_low = (value - value_high.astype(jnp.float32)).astype(jnp.bfloat16)
    stage[...] = jnp.zeros_like(stage)
    inverse[...] = jnp.zeros_like(inverse)
    lane = lane_iota((1, 128))
    cell_z, cell_x, cell_y = lane >> 6, lane >> 3 & 7, lane & 7

    def first_copy(j):
        a, b, c = lax.div(j, 25), lax.rem(lax.div(j, 5), 5), lax.rem(j, 5)
        keep_x = cell_x + jnp.where(a < 4, 7, 0) >= 7
        keep_y = cell_y + jnp.where(b < 4, 7, 0) >= 7
        keep_z = cell_z + jnp.where(c < 4, 1, 0) >= 1
        kept = jnp.where(keep_x & keep_y & keep_z, 1, 0)
        return kept * (j + 1), kept * lane

    def step(i, carry):
        j = 2 * i
        slot_low = jnp.concatenate([low[pl.ds(j, 1), :], low[pl.ds(j + 1, 1), :]], axis=1)
        slot_high = jnp.concatenate([high[pl.ds(j, 1), :], high[pl.ds(j + 1, 1), :]], axis=1)
        one_hot = jnp.where(row_iota((256, 256)) == slot_low, 1.0, 0.0).astype(jnp.bfloat16)
        product = jnp.dot(value_high, one_hot, preferred_element_type=jnp.float32)
        product = product + jnp.dot(value_low, one_hot, preferred_element_type=jnp.float32)
        total = jnp.zeros((group, 256), jnp.float32)
        for chunk in range(chunks):
            total = total + jnp.where(
                slot_high == chunk, product[group * chunk:group * chunk + group], 0.0
            )
        for part in range(2):
            row = 8 * lax.div(j + part, 5) + lax.rem(j + part, 5)
            stage[pl.ds(pl.multiple_of(row * group, 8), group), :] = total[:, 128 * part:128 * part + 128]
        row_a, cell_a = first_copy(j)
        row_b, cell_b = first_copy(j + 1)
        row_code = jnp.concatenate([row_a, row_b], axis=1)
        cell_code = jnp.concatenate([cell_a, cell_b], axis=1)
        here = row_iota((40, 256)) == slot_high
        codes = jnp.concatenate(
            [jnp.where(here, row_code, 0), jnp.where(here, cell_code, 0)], axis=0
        ).astype(jnp.float32).astype(jnp.bfloat16)
        inverse[...] += lax.dot_general(
            codes, one_hot, (((1,), (1,)), ((), ())), preferred_element_type=jnp.float32
        )
        return carry

    lax.fori_loop(0, HALF, step, 0)
    for v in range(vectors + 1):
        column = stage[pl.ds(v, ROWS, stride=group), :]
        nodal[ROWS * v:ROWS * v + ROWS, :] = column
        top = stage[pl.ds(4 * group + v, 25, stride=8 * group), :]
        top_high = top.astype(jnp.bfloat16).astype(jnp.float32)
        both = jnp.where(lane >= 64, top - top_high, pltpu.roll(top_high, 64, 1))
        face[32 * v:32 * v + 32, :] = jnp.concatenate(
            [both, jnp.zeros((7, 128), jnp.float32)], axis=0
        ).astype(jnp.bfloat16)


def shared_sums(terms):
    lane = lane_iota((8, 128))
    row = row_iota((8, 128))
    cell_z, cell_x, cell_y = lane >> 6, lane >> 3 & 7, lane & 7
    block = [terms[8 * k:8 * k + 8] for k in range(25)]
    for b in range(5):
        first, last = block[b], block[20 + b]
        block[b] = first + jnp.where(cell_x > 0, pltpu.roll(last, 8, 1), 0.0)
        block[20 + b] = last + jnp.where(cell_x < 7, pltpu.roll(first, 120, 1), 0.0)
    for a in range(5):
        first, last = block[5 * a], block[5 * a + 4]
        block[5 * a] = first + jnp.where(cell_y > 0, pltpu.roll(last, 1, 1), 0.0)
        block[5 * a + 4] = last + jnp.where(cell_y < 7, pltpu.roll(first, 127, 1), 0.0)
    joined = ((row == 0) & (cell_z == 1)) | ((row == 4) & (cell_z == 0))
    for k in range(25):
        other = pltpu.roll(pltpu.roll(block[k], 64, 1), 4, 0)
        block[k] = block[k] + jnp.where(joined, other, 0.0)
    return jnp.concatenate(block, axis=0)


def cell_operator(pair, stiffness, cell_data):
    values = jnp.concatenate(pair, axis=1).astype(jnp.bfloat16)
    stiff = jnp.dot(stiffness, values, preferred_element_type=jnp.float32)
    coefficient, kinetic = cell_data[:ROWS], cell_data[ROWS:ROWS + 1]
    results = []
    for part in range(2):
        columns = slice(128 * part, 128 * part + 128)
        low = values[:, columns].astype(jnp.float32)
        results.append(shared_sums(kinetic * stiff[:, columns] + coefficient * low))
    return results


def face_rows(sums_ref, start):
    lane = lane_iota((1, 128))
    bottom = sums_ref[pl.ds(start, 25, stride=8), :]
    top = sums_ref[pl.ds(start + 4, 25, stride=8), :]
    rows = jnp.where(lane < 64, bottom, top)
    return jnp.concatenate([rows, jnp.zeros((7, 128), jnp.float32)], axis=0).astype(jnp.bfloat16)


def first_kernel(nodal_in, ghost, stiffness, cell_data, nodal, sums, face):
    lane = lane_iota((1, 128))
    vectors = (nodal_in.shape[0] // ROWS) - 1
    nodal[...] = nodal_in[...]
    for v in range(vectors + 1):
        got = ghost[32 * v:32 * v + 32, :].astype(jnp.float32)[:25]
        value = got + pltpu.roll(got, 64, 1)
        old = nodal[pl.ds(ROWS * v, 25, stride=8), :]
        nodal[pl.ds(ROWS * v, 25, stride=8), :] = jnp.where(lane < 64, value, old)

    def step(i, carry):
        start = [pl.multiple_of(2 * ROWS * i, 8), pl.multiple_of(2 * ROWS * i + ROWS, 8)]
        pair = [nodal[pl.ds(start[k], ROWS), :] for k in range(2)]
        result = cell_operator(pair, stiffness[...], cell_data[...])
        for k in range(2):
            sums[pl.ds(start[k], ROWS), :] = result[k]
        return carry

    lax.fori_loop(0, vectors // 2, step, 0)
    for v in range(vectors):
        face[32 * v:32 * v + 32, :] = face_rows(sums, ROWS * v)


def add_faces(sums, v, from_above, from_below):
    lane = lane_iota((1, 128))
    if from_above is not None:
        got = pltpu.roll(from_above[32 * v:32 * v + 32, :].astype(jnp.float32)[:25], 64, 1)
        sums[pl.ds(ROWS * v + 4, 25, stride=8), :] += jnp.where(lane >= 64, got, 0.0)
    if from_below is not None:
        got = pltpu.roll(from_below[32 * v:32 * v + 32, :].astype(jnp.float32)[:25], 64, 1)
        sums[pl.ds(ROWS * v, 25, stride=8), :] += jnp.where(lane < 64, got, 0.0)


def second_kernel(
    bounds, nodal, sums_in, from_above, from_below, stiffness, cell_data, degree, sums, face, work
):
    vectors = (nodal.shape[0] // ROWS) - 1
    center, halfwidth = bounds[0], bounds[1]
    work[...] = sums_in[...]
    for v in range(vectors):
        add_faces(work, v, from_above, from_below)
    mass = nodal[ROWS * vectors:ROWS * vectors + ROWS, :]
    squared = mass * mass

    def step(i, carry):
        start = [pl.multiple_of(2 * ROWS * i, 8), pl.multiple_of(2 * ROWS * i + ROWS, 8)]
        pair = []
        for k in range(2):
            here = pl.ds(start[k], ROWS)
            pair.append((squared * work[here, :] - center * nodal[here, :]) / halfwidth)
            degree[here, :] = pair[k]
        result = cell_operator(pair, stiffness[...], cell_data[...])
        for k in range(2):
            sums[pl.ds(start[k], ROWS), :] = result[k]
        return carry

    lax.fori_loop(0, vectors // 2, step, 0)
    for v in range(vectors):
        face[32 * v:32 * v + 32, :] = face_rows(sums, ROWS * v)


def last_kernel(bounds, nodal, degree, sums_in, from_above, inverse, wave, rounded, work, spread_out):
    vectors = wave.shape[0]
    chunks = wave.shape[1] // 256
    center, halfwidth = bounds[0], bounds[1]
    work[...] = sums_in[...]
    mass = nodal[ROWS * vectors:ROWS * vectors + ROWS, :]
    squared = mass * mass
    unscale = 1.0 / jnp.where(mass == 0.0, 1.0, mass)
    spread_out[125 * vectors:126 * vectors, :] = jnp.zeros((vectors, 128), jnp.float32)
    for v in range(vectors):
        add_faces(work, v, from_above, None)
        here = slice(ROWS * v, ROWS * v + ROWS)
        second = 2.0 * (squared * work[here, :] - center * degree[here, :]) / halfwidth - nodal[here, :]
        second = second * unscale
        for k in range(25):
            spread_out[pl.ds(5 * k * vectors + v, 5, stride=vectors), :] = second[8 * k:8 * k + 5]
    table = jnp.concatenate(
        [spread_out[:HALF * vectors, :], spread_out[HALF * vectors:2 * HALF * vectors, :]], axis=1
    ).astype(jnp.bfloat16)
    for chunk in range(chunks):
        columns = slice(256 * chunk, 256 * chunk + 256)
        row_code = inverse[chunk:chunk + 1, :].astype(jnp.int32) - 1
        cell_code = inverse[40 + chunk:41 + chunk, :].astype(jnp.int32)
        second_half = row_code >= HALF
        column = jnp.where(second_half, cell_code + 128, cell_code)
        row = jnp.where(second_half, row_code - HALF, row_code)
        one_hot = jnp.where(row_iota((256, 256)) == column, 1.0, 0.0).astype(jnp.bfloat16)
        product = jnp.dot(table, one_hot, preferred_element_type=jnp.float32)
        vector = wave[:, columns]
        one = -center * vector / halfwidth
        unused = -2.0 * center * one / halfwidth - vector
        total = jnp.where(row_code < 0, unused, 0.0)
        for k in range(HALF):
            total = total + jnp.where(row == k, product[vectors * k:vectors * k + vectors], 0.0)
        rounded[:, columns] = total.astype(jnp.bfloat16)


def local_call(kernel, out_shape, scratch=(), smem_first=False, inputs=0):
    specs = [pl.BlockSpec(memory_space=pltpu.VMEM)] * inputs
    if smem_first:
        specs[0] = pl.BlockSpec(memory_space=pltpu.SMEM)
    return pl.pallas_call(
        kernel,
        out_shape=out_shape,
        in_specs=specs,
        out_specs=jax.tree.map(lambda _: pl.BlockSpec(memory_space=pltpu.VMEM), out_shape),
        scratch_shapes=list(scratch),
        compiler_params=pltpu.CompilerParams(vmem_limit_bytes=VMEM_BYTES),
    )


def per_device(
    wave_block,
    connectivity,
    send_list,
    levels,
    live_cells,
    potential,
    mass_scale,
    center,
    halfwidth,
    earlier_vectors,
):
    stiffness, quadrature, spread, reorder = fixed_tables()
    stiffness = jnp.asarray(stiffness).astype(jnp.bfloat16)
    vectors, owned = wave_block.shape
    nodes, cells = connectivity.shape
    group = vectors + 8
    cell_size = jnp.exp2(-levels.astype(jnp.float32))
    in_use = (jnp.arange(cells, dtype=jnp.int32) < live_cells[0]).astype(jnp.float32)
    kinetic = cell_size / 4.0 * in_use
    volume = cell_size**3 / 8.0 * in_use
    coefficient = volume[None, :] * jnp.asarray(quadrature)[:, None] * potential
    cell_data = jnp.concatenate([coefficient, kinetic[None], jnp.zeros((2, cells), jnp.float32)], 0)
    padding = ((0, 128 - nodes), (0, 0))
    conn_low = jnp.pad(connectivity & 255, padding).astype(jnp.bfloat16)
    conn_high = jnp.pad(connectivity >> 8, padding, constant_values=63).astype(jnp.bfloat16)
    f32, bf16 = jnp.float32, jnp.bfloat16
    shape = jax.ShapeDtypeStruct
    bounds = jnp.stack([center, halfwidth])

    nodal, face, inverse, cell_data = local_call(
        gather_kernel,
        (
            shape(((vectors + 1) * ROWS, 128), f32),
            shape(((vectors + 1) * 32, 128), bf16),
            shape((80, 256), f32),
            shape((208, 128), f32),
        ),
        [
            pltpu.VMEM((group * owned // 256, 256), f32),
            pltpu.VMEM((128, 128), jnp.int32),
            pltpu.VMEM((128, 128), jnp.int32),
            pltpu.VMEM((ROWS * group + group * 8, 128), f32),
        ],
        inputs=7,
    )(wave_block, mass_scale[None], conn_high, conn_low, cell_data, jnp.asarray(spread), jnp.asarray(reorder))
    ghost = passed_along(face, "cells", 1)
    nodal, sums, face = local_call(
        first_kernel,
        (
            shape(((vectors + 1) * ROWS, 128), f32),
            shape((vectors * ROWS, 128), f32),
            shape((vectors * 32, 128), bf16),
        ),
        inputs=4,
    )(nodal, ghost, stiffness, cell_data)
    from_above = passed_along(face, "cells", -1)
    from_below = passed_along(face, "cells", 1)
    degree, sums, face = local_call(
        second_kernel,
        (
            shape((vectors * ROWS, 128), f32),
            shape((vectors * ROWS, 128), f32),
            shape((vectors * 32, 128), bf16),
        ),
        [pltpu.VMEM((vectors * ROWS, 128), f32)],
        smem_first=True,
        inputs=7,
    )(bounds, nodal, sums, from_above, from_below, stiffness, cell_data)
    from_above = passed_along(face, "cells", -1)
    rounded = local_call(
        last_kernel,
        shape((vectors, owned), bf16),
        [
            pltpu.VMEM((vectors * ROWS, 128), f32),
            pltpu.VMEM((2 * HALF * vectors, 128), f32),
        ],
        smem_first=True,
        inputs=7,
    )(bounds, nodal, degree, sums, from_above, inverse, wave_block)

    quarter = lax.all_to_all(rounded, "vecs", split_axis=1, concat_axis=0, tiled=True)
    row_share = earlier_vectors.shape[0] // lax.axis_size(("cells", "vecs"))
    partial_sum = lax.dot_general(
        earlier_vectors, quarter, (((1,), (1,)), ((), ())), preferred_element_type=jnp.float32
    )
    projections = lax.psum(partial_sum, ("cells", "vecs"))
    filtered = quarter.astype(jnp.float32) - lax.dot_general(
        projections.astype(jnp.bfloat16),
        earlier_vectors,
        (((0,), (0,)), ((), ())),
        preferred_element_type=jnp.float32,
    )
    own_rows = lax.dynamic_slice_in_dim(
        projections, lax.axis_index(("cells", "vecs")) * row_share, row_share, 0
    )
    return (filtered, own_rows)


def solution(mesh):
    in_specs = (
        P("vecs", "cells"),
        P(None, "cells"),
        P("cells"),
        P("cells"),
        P("cells"),
        P(None, "cells"),
        P("cells"),
        P(),
        P(),
        P(None, ("cells", "vecs")),
    )
    out_specs = (P(None, ("cells", "vecs")), P(("cells", "vecs"), None))
    return jax.shard_map(
        per_device, mesh=mesh, in_specs=in_specs, out_specs=out_specs, check_vma=False
    )
```

```python
import functools
import math

import jax
import jax.numpy as jnp
import numpy as np
from jax import lax
from jax.experimental import pallas as pl
from jax.experimental.pallas import tpu as pltpu
from jax.sharding import PartitionSpec as P

ROWS = 200
GATHERED = 72
VMEM_BYTES = 48 * 1024 * 1024


def passed_along(value, axis, steps):
    count = lax.axis_size(axis)
    leading, last = (max(0, -steps), min(count, count - steps))
    return lax.ppermute(value, axis, [(source, source + steps) for source in range(leading, last)])


def gll_tables():
    root_value = math.sqrt(3.0 / 7.0)
    points = np.array([-1.0, -root_value, 0.0, root_value, 1.0])
    weights = np.array([0.1, 49.0 / 90.0, 32.0 / 45.0, 49.0 / 90.0, 0.1])
    barycentric = np.ones(5)
    for node_index in range(5):
        for other_node in range(5):
            if other_node != node_index:
                barycentric[node_index] = barycentric[node_index] / (
                    points[node_index] - points[other_node]
                )
    derivative = np.zeros((5, 5))
    for row_index in range(5):
        for col_index in range(5):
            if row_index != col_index:
                derivative[row_index, col_index] = (
                    barycentric[col_index]
                    / barycentric[row_index]
                    / (points[row_index] - points[col_index])
                )
        derivative[row_index, row_index] = -np.sum(derivative[row_index])
    mass_one = np.zeros((5, 5))
    for node_index in range(5):
        mass_one[node_index, node_index] = weights[node_index]
    laplace_one = derivative.T @ mass_one @ derivative
    stiffness = (
        np.kron(np.kron(laplace_one, mass_one), mass_one)
        + np.kron(np.kron(mass_one, laplace_one), mass_one)
        + np.kron(np.kron(mass_one, mass_one), laplace_one)
    )
    quadrature = np.kron(np.kron(weights, weights), weights)
    return (stiffness.astype(np.float32), quadrature.astype(np.float32))


def fixed_tables():
    stiffness, quadrature = gll_tables()
    spread = np.zeros((208, 128), np.float32)
    for j in range(125):
        spread[8 * (j // 5) + j % 5, j] = 1.0
    spread[200, 125] = 1.0
    padded = spread[:200, :125] @ stiffness @ spread[:200, :125].T
    reorder = np.zeros((128, 128), np.float32)
    for rank in range(128):
        bit = [rank >> k & 1 for k in range(7)]
        x = bit[0] + 2 * bit[3] + 4 * bit[5]
        y = bit[1] + 2 * bit[4] + 4 * bit[6]
        reorder[rank, 64 * bit[2] + 8 * x + y] = 1.0
    return padded, quadrature, spread, reorder


def lane_iota(shape):
    return lax.broadcasted_iota(jnp.int32, shape, 1)


def row_iota(shape):
    return lax.broadcasted_iota(jnp.int32, shape, 0)


def blocks_of(value):
    return [value[8 * k:8 * k + 8] for k in range(value.shape[0] // 8)]


def pack_edges(block, nothing):
    lane = lane_iota((8, 128))
    cell_x, cell_y = lane >> 3 & 7, lane & 7
    edge_x = jnp.full((8, 128), nothing, block[0].dtype)
    edge_y = edge_x
    for b in range(4):
        edge_x = jnp.where(cell_x == b, pltpu.roll(block[20 + b], 128 - 8 * (7 - b), 1), edge_x)
    corner = (cell_x == 4) & (cell_y == 7)
    edge_x = jnp.where(corner, pltpu.roll(block[24], 128 - 24, 1), edge_x)
    for a in range(4):
        edge_y = jnp.where(cell_y == a, pltpu.roll(block[5 * a + 4], 128 - (7 - a), 1), edge_y)
    return edge_x, edge_y


def fill_copies(block):
    lane = lane_iota((8, 128))
    row = row_iota((8, 128))
    cell_z, cell_x, cell_y = lane >> 6, lane >> 3 & 7, lane & 7
    edge_x, edge_y = block[25], block[26]
    block = block[:25]
    for b in range(4):
        last = pltpu.roll(edge_x, 8 * (7 - b), 1) if b < 7 else edge_x
        block[20 + b] = jnp.where(cell_x < 7, pltpu.roll(block[b], 120, 1), last)
    for a in range(4):
        last = pltpu.roll(edge_y, 7 - a, 1)
        block[5 * a + 4] = jnp.where(cell_y < 7, pltpu.roll(block[5 * a], 127, 1), last)
    last = jnp.where(cell_y < 7, pltpu.roll(block[20], 127, 1), pltpu.roll(edge_x, 24, 1))
    block[24] = jnp.where(cell_x < 7, pltpu.roll(block[4], 120, 1), last)
    joined = (row == 0) & (cell_z == 1)
    for k in range(25):
        other = pltpu.roll(pltpu.roll(block[k], 64, 1), 4, 0)
        block[k] = jnp.where(joined, other, block[k])
    return jnp.concatenate(block, axis=0)


def gather_kernel(
    wave, mass, conn_high, conn_low, cell_data, spread, reorder,
    nodal, face, inverse, cell_out, packed, low, high, stage,
):
    chunks = wave.shape[1] // 256
    vectors = wave.shape[0]
    group = vectors + 8
    order = reorder[...]
    order_low = order.astype(jnp.bfloat16)
    spread_low = spread[:ROWS, :].astype(jnp.bfloat16)
    for source, target, nothing in ((conn_high, high, 63), (conn_low, low, 0)):
        spaced = jnp.dot(spread_low, source[...], preferred_element_type=jnp.float32)
        ordered = jnp.dot(spaced.astype(jnp.bfloat16), order_low, preferred_element_type=jnp.float32)
        ordered = ordered.astype(jnp.int32)
        target[:ROWS, :] = ordered
        edge_x, edge_y = pack_edges(blocks_of(ordered), nothing)
        target[ROWS:ROWS + 8, :] = edge_x
        target[ROWS + 8:ROWS + 16, :] = edge_y
    exact = lax.Precision.HIGHEST
    ordered = jnp.dot(cell_data[...], order, precision=exact, preferred_element_type=jnp.float32)
    cell_out[...] = jnp.dot(spread[...], ordered, precision=exact, preferred_element_type=jnp.float32)
    for chunk in range(chunks):
        columns = slice(256 * chunk, 256 * chunk + 256)
        scale = mass[:, columns]
        packed[group * chunk:group * chunk + vectors, :] = wave[:, columns] * scale
        packed[group * chunk + vectors:group * chunk + group, :] = jnp.broadcast_to(scale, (8, 256))
    value = packed[...]
    value_high = value.astype(jnp.bfloat16)
    value_low = (value - value_high.astype(jnp.float32)).astype(jnp.bfloat16)
    both = jnp.concatenate([value_high, value_low], axis=1)
    stage[...] = jnp.zeros_like(stage)
    inverse[...] = jnp.zeros_like(inverse)
    lane = lane_iota((1, 128))
    pair_lane = lane_iota((1, 256))

    def step(i, carry):
        at = lax.div(i, 2)
        block = jnp.where(at < 16, 5 * lax.div(at, 4) + lax.rem(at, 4), at + 9)
        row = 8 * block + 1 + 2 * lax.rem(i, 2)
        slot_low = jnp.concatenate([low[pl.ds(row, 1), :], low[pl.ds(row + 1, 1), :]], axis=1)
        slot_high = jnp.concatenate([high[pl.ds(row, 1), :], high[pl.ds(row + 1, 1), :]], axis=1)
        one_hot = jnp.where(row_iota((256, 256)) == slot_low, 1.0, 0.0).astype(jnp.bfloat16)
        twice = jnp.concatenate([one_hot, one_hot], axis=0)
        product = jnp.dot(both, twice, preferred_element_type=jnp.float32)
        total = jnp.zeros((group, 256), jnp.float32)
        for chunk in range(chunks):
            total = total + jnp.where(
                slot_high == chunk, product[group * chunk:group * chunk + group], 0.0
            )
        for part in range(2):
            start = pl.multiple_of((row + part) * group, 8)
            stage[pl.ds(start, group), :] = total[:, 128 * part:128 * part + 128]
        row_code = 2 * i + 1 + (pair_lane >> 7)
        cell_code = pair_lane & 127
        here = row_iota((40, 256)) == slot_high
        codes = jnp.concatenate(
            [jnp.where(here, row_code, 0), jnp.where(here, cell_code, 0)], axis=0
        ).astype(jnp.float32).astype(jnp.bfloat16)
        inverse[...] += lax.dot_general(
            codes, one_hot, (((1,), (1,)), ((), ())), preferred_element_type=jnp.float32
        )
        return carry

    lax.fori_loop(0, GATHERED // 2, step, 0)
    for v in range(vectors + 1):
        column = fill_copies(blocks_of(stage[pl.ds(v, ROWS + 16, stride=group), :]))
        nodal[ROWS * v:ROWS * v + ROWS, :] = column
        top = nodal[pl.ds(ROWS * v + 4, 25, stride=8), :]
        top_high = top.astype(jnp.bfloat16).astype(jnp.float32)
        parts = jnp.where(lane >= 64, top - top_high, pltpu.roll(top_high, 64, 1))
        face[32 * v:32 * v + 32, :] = jnp.concatenate(
            [parts, jnp.zeros((7, 128), jnp.float32)], axis=0
        ).astype(jnp.bfloat16)


def shared_sums(terms):
    lane = lane_iota((8, 128))
    row = row_iota((8, 128))
    cell_z, cell_x, cell_y = lane >> 6, lane >> 3 & 7, lane & 7
    block = [terms[8 * k:8 * k + 8] for k in range(25)]
    for b in range(5):
        first, last = block[b], block[20 + b]
        block[b] = first + jnp.where(cell_x > 0, pltpu.roll(last, 8, 1), 0.0)
        block[20 + b] = last + jnp.where(cell_x < 7, pltpu.roll(first, 120, 1), 0.0)
    for a in range(5):
        first, last = block[5 * a], block[5 * a + 4]
        block[5 * a] = first + jnp.where(cell_y > 0, pltpu.roll(last, 1, 1), 0.0)
        block[5 * a + 4] = last + jnp.where(cell_y < 7, pltpu.roll(first, 127, 1), 0.0)
    joined = ((row == 0) & (cell_z == 1)) | ((row == 4) & (cell_z == 0))
    for k in range(25):
        other = pltpu.roll(pltpu.roll(block[k], 64, 1), 4, 0)
        block[k] = block[k] + jnp.where(joined, other, 0.0)
    return jnp.concatenate(block, axis=0)


def cell_operator(pair, stiffness, cell_data):
    values = jnp.concatenate(pair, axis=1).astype(jnp.bfloat16)
    stiff = jnp.dot(stiffness, values, preferred_element_type=jnp.float32)
    coefficient, kinetic = cell_data[:ROWS], cell_data[ROWS:ROWS + 1]
    results = []
    for part in range(2):
        columns = slice(128 * part, 128 * part + 128)
        low = values[:, columns].astype(jnp.float32)
        results.append(shared_sums(kinetic * stiff[:, columns] + coefficient * low))
    return results


def face_rows(sums_ref, start):
    lane = lane_iota((1, 128))
    bottom = sums_ref[pl.ds(start, 25, stride=8), :]
    top = sums_ref[pl.ds(start + 4, 25, stride=8), :]
    rows = jnp.where(lane < 64, bottom, top)
    return jnp.concatenate([rows, jnp.zeros((7, 128), jnp.float32)], axis=0).astype(jnp.bfloat16)


def first_kernel(nodal_in, ghost, stiffness, cell_data, nodal, sums, face):
    lane = lane_iota((1, 128))
    vectors = (nodal_in.shape[0] // ROWS) - 1
    nodal[...] = nodal_in[...]
    for v in range(vectors + 1):
        got = ghost[32 * v:32 * v + 32, :].astype(jnp.float32)[:25]
        value = got + pltpu.roll(got, 64, 1)
        old = nodal[pl.ds(ROWS * v, 25, stride=8), :]
        nodal[pl.ds(ROWS * v, 25, stride=8), :] = jnp.where(lane < 64, value, old)

    def step(i, carry):
        start = [pl.multiple_of(2 * ROWS * i, 8), pl.multiple_of(2 * ROWS * i + ROWS, 8)]
        pair = [nodal[pl.ds(start[k], ROWS), :] for k in range(2)]
        result = cell_operator(pair, stiffness[...], cell_data[...])
        for k in range(2):
            sums[pl.ds(start[k], ROWS), :] = result[k]
        return carry

    lax.fori_loop(0, vectors // 2, step, 0)
    for v in range(vectors):
        face[32 * v:32 * v + 32, :] = face_rows(sums, ROWS * v)


def add_faces(sums, v, from_above, from_below):
    lane = lane_iota((1, 128))
    if from_above is not None:
        got = pltpu.roll(from_above[32 * v:32 * v + 32, :].astype(jnp.float32)[:25], 64, 1)
        sums[pl.ds(ROWS * v + 4, 25, stride=8), :] += jnp.where(lane >= 64, got, 0.0)
    if from_below is not None:
        got = pltpu.roll(from_below[32 * v:32 * v + 32, :].astype(jnp.float32)[:25], 64, 1)
        sums[pl.ds(ROWS * v, 25, stride=8), :] += jnp.where(lane < 64, got, 0.0)


def second_kernel(
    bounds, nodal, sums_in, from_above, from_below, stiffness, cell_data, degree, sums, face, work
):
    vectors = (nodal.shape[0] // ROWS) - 1
    center, halfwidth = bounds[0], bounds[1]
    work[...] = sums_in[...]
    for v in range(vectors):
        add_faces(work, v, from_above, from_below)
    mass = nodal[ROWS * vectors:ROWS * vectors + ROWS, :]
    squared = mass * mass

    def step(i, carry):
        start = [pl.multiple_of(2 * ROWS * i, 8), pl.multiple_of(2 * ROWS * i + ROWS, 8)]
        pair = []
        for k in range(2):
            here = pl.ds(start[k], ROWS)
            pair.append((squared * work[here, :] - center * nodal[here, :]) / halfwidth)
            degree[here, :] = pair[k]
        result = cell_operator(pair, stiffness[...], cell_data[...])
        for k in range(2):
            sums[pl.ds(start[k], ROWS), :] = result[k]
        return carry

    lax.fori_loop(0, vectors // 2, step, 0)
    for v in range(vectors):
        face[32 * v:32 * v + 32, :] = face_rows(sums, ROWS * v)


def last_kernel(bounds, nodal, degree, sums_in, from_above, inverse, wave, rounded, work, spread_out):
    vectors = wave.shape[0]
    chunks = wave.shape[1] // 256
    center, halfwidth = bounds[0], bounds[1]
    work[...] = sums_in[...]
    mass = nodal[ROWS * vectors:ROWS * vectors + ROWS, :]
    squared = mass * mass
    unscale = 1.0 / jnp.where(mass == 0.0, 1.0, mass)
    for v in range(vectors):
        add_faces(work, v, from_above, None)
        here = slice(ROWS * v, ROWS * v + ROWS)
        second = 2.0 * (squared * work[here, :] - center * degree[here, :]) / halfwidth - nodal[here, :]
        block = blocks_of(second * unscale)
        kept = [block[5 * a + b] for a in range(4) for b in range(4)]
        for k, part in enumerate(kept + list(pack_edges(block, 0.0))):
            spread_out[pl.ds(4 * k * vectors + v, 4, stride=vectors), :] = part[1:5]
    middle = GATHERED // 2 * vectors
    table = jnp.concatenate(
        [spread_out[:middle, :], spread_out[middle:2 * middle, :]], axis=1
    ).astype(jnp.bfloat16)
    for chunk in range(chunks):
        columns = slice(256 * chunk, 256 * chunk + 256)
        row_code = inverse[chunk:chunk + 1, :].astype(jnp.int32) - 1
        cell_code = inverse[40 + chunk:41 + chunk, :].astype(jnp.int32)
        second_half = row_code >= GATHERED // 2
        column = jnp.where(second_half, cell_code + 128, cell_code)
        row = jnp.where(second_half, row_code - GATHERED // 2, row_code)
        one_hot = jnp.where(row_iota((256, 256)) == column, 1.0, 0.0).astype(jnp.bfloat16)
        product = jnp.dot(table, one_hot, preferred_element_type=jnp.float32)
        vector = wave[:, columns]
        one = -center * vector / halfwidth
        unused = -2.0 * center * one / halfwidth - vector
        total = jnp.where(row_code < 0, unused, 0.0)
        for k in range(GATHERED // 2):
            total = total + jnp.where(row == k, product[vectors * k:vectors * k + vectors], 0.0)
        rounded[:, columns] = total.astype(jnp.bfloat16)


def mesh_id(peer, others):
    return (lax.div(peer, others), lax.rem(peer, others))


def meet_all(me, count, others):
    barrier = pltpu.get_barrier_semaphore()

    def greet(k, carry):
        peer = lax.rem(me + k, count)
        pl.semaphore_signal(
            barrier, inc=1, device_id=mesh_id(peer, others), device_id_type=pl.DeviceIdType.MESH
        )
        return carry

    lax.fori_loop(1, count, greet, 0)
    pl.semaphore_wait(barrier, count - 1)


def wait_bytes(ref, semaphore):
    pltpu.make_async_copy(ref, ref, semaphore).wait()


def projection_kernel(
    rows_of, others, rounded, earlier, filtered, own_rows,
    held, quarter, partial, to_send, received, own_low, gathered, low_rows,
    load_sem, swap_send, swap_recv, sum_send, sum_recv, all_send, all_recv,
):
    count = rows_of * others
    mine, along = lax.axis_index("vecs"), lax.axis_index("cells")
    me = along * others + mine
    vectors = rounded.shape[0]
    width = earlier.shape[1]
    share = earlier.shape[0] // count
    half = share // 2
    parts = load_sem.shape[0]
    depth = earlier.shape[0] // parts
    blocks = depth // share
    first_part = lax.div(along * parts, rows_of) + 1
    columns = others * vectors
    loads = []
    for k in range(parts):
        here = pl.ds(pl.multiple_of(lax.rem(first_part + k, parts) * depth, depth), depth)
        loads.append(pltpu.make_async_copy(earlier.at[here], held.at[here], load_sem.at[k]))
        loads[k].start()
    meet_all(me, count, others)
    for k in range(1, others):
        peer = lax.rem(mine + k, others)
        source = rounded.at[:, pl.ds(pl.multiple_of(peer * width, 128), width)]
        pltpu.make_async_remote_copy(
            source, quarter.at[mine], swap_send, swap_recv,
            device_id=(along, peer), device_id_type=pl.DeviceIdType.MESH,
        ).start()
    quarter[mine] = rounded[:, pl.ds(pl.multiple_of(mine * width, 128), width)]
    wait_bytes(quarter.at[pl.ds(0, others - 1)], swap_recv)
    vectors_here = quarter[...].reshape(columns, width)
    for k in range(parts):
        part = lax.rem(first_part + k, parts)
        loads[k].wait()
        result = lax.dot_general(
            held[pl.ds(pl.multiple_of(part * depth, depth), depth), :], vectors_here,
            (((1,), (1,)), ((), ())), preferred_element_type=jnp.float32,
        )
        for t in range(blocks):
            piece = result[share * t:share * t + share]
            piece = jnp.concatenate([piece[:half], piece[half:]], axis=1)
            partial[part * blocks + t] = piece
            to_send[part * blocks + t] = piece.astype(jnp.bfloat16)
        for t in range(blocks):
            owner = part * blocks + lax.rem(me + t, blocks)
            slot = lax.rem(owner - me + count, count) - 1

            @pl.when(owner != me)
            def _():
                pltpu.make_async_remote_copy(
                    to_send.at[owner], received.at[slot], sum_send, sum_recv,
                    device_id=mesh_id(owner, others), device_id_type=pl.DeviceIdType.MESH,
                ).start()

    wait_bytes(received, sum_recv)
    total = partial[me]
    for k in range(count - 1):
        total = total + received[k].astype(jnp.float32)
    own_rows[...] = jnp.concatenate([total[:, :columns], total[:, columns:]], axis=0)
    own_low[...] = total.astype(jnp.bfloat16)
    gathered[me] = own_low[...]
    for k in range(1, count):
        peer = lax.rem(me + k, count)
        pltpu.make_async_remote_copy(
            own_low, gathered.at[me], all_send, all_recv,
            device_id=mesh_id(peer, others), device_id_type=pl.DeviceIdType.MESH,
        ).start()
    wait_bytes(gathered.at[pl.ds(0, count - 1)], all_recv)
    for k in range(count):
        piece = gathered[k]
        low_rows[share * k:share * k + half, :] = piece[:, :columns]
        low_rows[share * k + half:share * k + share, :] = piece[:, columns:]
    weights = low_rows[...].astype(jnp.float32).T.astype(jnp.bfloat16)
    step = 256
    for start in range(0, width, step):
        here = slice(start, start + step)
        taken = jnp.dot(weights, held[:, here], preferred_element_type=jnp.float32)
        filtered[:, here] = vectors_here[:, here].astype(jnp.float32) - taken
    wait_bytes(quarter.at[pl.ds(0, others - 1)], swap_send)
    wait_bytes(received, sum_send)
    wait_bytes(gathered.at[pl.ds(0, count - 1)], all_send)


def project_out(rounded, earlier_vectors):
    along, others = lax.axis_size("cells"), lax.axis_size("vecs")
    count = along * others
    vectors = rounded.shape[0]
    depth, width = earlier_vectors.shape
    share, columns = depth // count, vectors * others
    bf16, f32 = jnp.bfloat16, jnp.float32
    dma = pltpu.SemaphoreType.DMA
    return pl.pallas_call(
        functools.partial(projection_kernel, along, others),
        out_shape=(
            jax.ShapeDtypeStruct((columns, width), f32),
            jax.ShapeDtypeStruct((share, columns), f32),
        ),
        in_specs=[pl.BlockSpec(memory_space=pltpu.VMEM), pl.BlockSpec(memory_space=pl.ANY)],
        out_specs=(pl.BlockSpec(memory_space=pltpu.VMEM),) * 2,
        scratch_shapes=[
            pltpu.VMEM((depth, width), bf16),
            pltpu.VMEM((others, vectors, width), bf16),
            pltpu.VMEM((count, share // 2, 2 * columns), f32),
            pltpu.VMEM((count, share // 2, 2 * columns), bf16),
            pltpu.VMEM((count - 1, share // 2, 2 * columns), bf16),
            pltpu.VMEM((share // 2, 2 * columns), bf16),
            pltpu.VMEM((count, share // 2, 2 * columns), bf16),
            pltpu.VMEM((depth, columns), bf16),
            dma((4,)), dma, dma, dma, dma, dma, dma,
        ],
        compiler_params=pltpu.CompilerParams(
            collective_id=0, has_side_effects=True, vmem_limit_bytes=VMEM_BYTES
        ),
    )(rounded, earlier_vectors)


def local_call(kernel, out_shape, scratch=(), smem_first=False, inputs=0):
    specs = [pl.BlockSpec(memory_space=pltpu.VMEM)] * inputs
    if smem_first:
        specs[0] = pl.BlockSpec(memory_space=pltpu.SMEM)
    return pl.pallas_call(
        kernel,
        out_shape=out_shape,
        in_specs=specs,
        out_specs=jax.tree.map(lambda _: pl.BlockSpec(memory_space=pltpu.VMEM), out_shape),
        scratch_shapes=list(scratch),
        compiler_params=pltpu.CompilerParams(vmem_limit_bytes=VMEM_BYTES),
    )


def per_device(
    wave_block,
    connectivity,
    send_list,
    levels,
    live_cells,
    potential,
    mass_scale,
    center,
    halfwidth,
    earlier_vectors,
):
    stiffness, quadrature, spread, reorder = fixed_tables()
    stiffness = jnp.asarray(stiffness).astype(jnp.bfloat16)
    vectors, owned = wave_block.shape
    nodes, cells = connectivity.shape
    group = vectors + 8
    cell_size = jnp.exp2(-levels.astype(jnp.float32))
    in_use = (jnp.arange(cells, dtype=jnp.int32) < live_cells[0]).astype(jnp.float32)
    kinetic = cell_size / 4.0 * in_use
    volume = cell_size**3 / 8.0 * in_use
    coefficient = volume[None, :] * jnp.asarray(quadrature)[:, None] * potential
    cell_data = jnp.concatenate([coefficient, kinetic[None], jnp.zeros((2, cells), jnp.float32)], 0)
    padding = ((0, 128 - nodes), (0, 0))
    conn_low = jnp.pad(connectivity & 255, padding).astype(jnp.bfloat16)
    conn_high = jnp.pad(connectivity >> 8, padding, constant_values=63).astype(jnp.bfloat16)
    f32, bf16 = jnp.float32, jnp.bfloat16
    shape = jax.ShapeDtypeStruct
    bounds = jnp.stack([center, halfwidth])

    nodal, face, inverse, cell_data = local_call(
        gather_kernel,
        (
            shape(((vectors + 1) * ROWS, 128), f32),
            shape(((vectors + 1) * 32, 128), bf16),
            shape((80, 256), f32),
            shape((208, 128), f32),
        ),
        [
            pltpu.VMEM((group * owned // 256, 256), f32),
            pltpu.VMEM((ROWS + 16, 128), jnp.int32),
            pltpu.VMEM((ROWS + 16, 128), jnp.int32),
            pltpu.VMEM(((ROWS + 16) * group, 128), f32),
        ],
        inputs=7,
    )(wave_block, mass_scale[None], conn_high, conn_low, cell_data, jnp.asarray(spread), jnp.asarray(reorder))
    ghost = passed_along(face, "cells", 1)
    nodal, sums, face = local_call(
        first_kernel,
        (
            shape(((vectors + 1) * ROWS, 128), f32),
            shape((vectors * ROWS, 128), f32),
            shape((vectors * 32, 128), bf16),
        ),
        inputs=4,
    )(nodal, ghost, stiffness, cell_data)
    from_above = passed_along(face, "cells", -1)
    from_below = passed_along(face, "cells", 1)
    degree, sums, face = local_call(
        second_kernel,
        (
            shape((vectors * ROWS, 128), f32),
            shape((vectors * ROWS, 128), f32),
            shape((vectors * 32, 128), bf16),
        ),
        [pltpu.VMEM((vectors * ROWS, 128), f32)],
        smem_first=True,
        inputs=7,
    )(bounds, nodal, sums, from_above, from_below, stiffness, cell_data)
    from_above = passed_along(face, "cells", -1)
    rounded = local_call(
        last_kernel,
        shape((vectors, owned), bf16),
        [
            pltpu.VMEM((vectors * ROWS, 128), f32),
            pltpu.VMEM((GATHERED * vectors, 128), f32),
        ],
        smem_first=True,
        inputs=7,
    )(bounds, nodal, degree, sums, from_above, inverse, wave_block)

    share = earlier_vectors.shape[0] // lax.axis_size(("cells", "vecs"))
    if share % 32 == 0:
        return project_out(rounded, earlier_vectors)
    quarter = lax.all_to_all(rounded, "vecs", split_axis=1, concat_axis=0, tiled=True)
    row_share = earlier_vectors.shape[0] // lax.axis_size(("cells", "vecs"))
    partial_sum = lax.dot_general(
        earlier_vectors, quarter, (((1,), (1,)), ((), ())), preferred_element_type=jnp.float32
    )
    projections = lax.psum(partial_sum, ("cells", "vecs"))
    filtered = quarter.astype(jnp.float32) - lax.dot_general(
        projections.astype(jnp.bfloat16),
        earlier_vectors,
        (((0,), (0,)), ((), ())),
        preferred_element_type=jnp.float32,
    )
    own_rows = lax.dynamic_slice_in_dim(
        projections, lax.axis_index(("cells", "vecs")) * row_share, row_share, 0
    )
    return (filtered, own_rows)


def solution(mesh):
    in_specs = (
        P("vecs", "cells"),
        P(None, "cells"),
        P("cells"),
        P("cells"),
        P("cells"),
        P(None, "cells"),
        P("cells"),
        P(),
        P(),
        P(None, ("cells", "vecs")),
    )
    out_specs = (P(None, ("cells", "vecs")), P(("cells", "vecs"), None))
    return jax.shard_map(
        per_device, mesh=mesh, in_specs=in_specs, out_specs=out_specs, check_vma=False
    )
```

```python
import functools
import math

import jax
import jax.numpy as jnp
import numpy as np
from jax import lax
from jax.experimental import pallas as pl
from jax.experimental.pallas import tpu as pltpu
from jax.sharding import PartitionSpec as P

ROWS = 200
GATHERED = 72
VMEM_BYTES = 36 * 1024 * 1024


def gll_tables():
    root_value = math.sqrt(3.0 / 7.0)
    points = np.array([-1.0, -root_value, 0.0, root_value, 1.0])
    weights = np.array([0.1, 49.0 / 90.0, 32.0 / 45.0, 49.0 / 90.0, 0.1])
    barycentric = np.ones(5)
    for node_index in range(5):
        for other_node in range(5):
            if other_node != node_index:
                barycentric[node_index] = barycentric[node_index] / (
                    points[node_index] - points[other_node]
                )
    derivative = np.zeros((5, 5))
    for row_index in range(5):
        for col_index in range(5):
            if row_index != col_index:
                derivative[row_index, col_index] = (
                    barycentric[col_index]
                    / barycentric[row_index]
                    / (points[row_index] - points[col_index])
                )
        derivative[row_index, row_index] = -np.sum(derivative[row_index])
    mass_one = np.zeros((5, 5))
    for node_index in range(5):
        mass_one[node_index, node_index] = weights[node_index]
    laplace_one = derivative.T @ mass_one @ derivative
    stiffness = (
        np.kron(np.kron(laplace_one, mass_one), mass_one)
        + np.kron(np.kron(mass_one, laplace_one), mass_one)
        + np.kron(np.kron(mass_one, mass_one), laplace_one)
    )
    quadrature = np.kron(np.kron(weights, weights), weights)
    return (stiffness.astype(np.float32), quadrature.astype(np.float32))


def fixed_tables():
    stiffness, quadrature = gll_tables()
    spread = np.zeros((ROWS, 125), np.float32)
    for j in range(125):
        spread[8 * (j // 5) + j % 5, j] = 1.0
    padded = np.zeros((208, 256), np.float32)
    padded[:ROWS, :ROWS] = spread @ stiffness @ spread.T
    return padded, quadrature


def lane_iota(shape):
    return lax.broadcasted_iota(jnp.int32, shape, 1)


def row_iota(shape):
    return lax.broadcasted_iota(jnp.int32, shape, 0)


def blocks_of(value):
    return [value[8 * k:8 * k + 8] for k in range(value.shape[0] // 8)]


def pack_edges(block, nothing):
    lane = lane_iota((8, 128))
    cell_x, cell_y = lane >> 3 & 7, lane & 7
    edge_x = jnp.full((8, 128), nothing, block[0].dtype)
    edge_y = edge_x
    for b in range(4):
        edge_x = jnp.where(cell_x == b, pltpu.roll(block[20 + b], 128 - 8 * (7 - b), 1), edge_x)
    corner = (cell_x == 4) & (cell_y == 7)
    edge_x = jnp.where(corner, pltpu.roll(block[24], 128 - 24, 1), edge_x)
    for a in range(4):
        edge_y = jnp.where(cell_y == a, pltpu.roll(block[5 * a + 4], 128 - (7 - a), 1), edge_y)
    return edge_x, edge_y


def fill_copies(block):
    lane = lane_iota((8, 128))
    row = row_iota((8, 128))
    cell_z, cell_x, cell_y = lane >> 6, lane >> 3 & 7, lane & 7
    edge_x, edge_y = block[25], block[26]
    block = block[:25]
    for b in range(4):
        last = pltpu.roll(edge_x, 8 * (7 - b), 1) if b < 7 else edge_x
        block[20 + b] = jnp.where(cell_x < 7, pltpu.roll(block[b], 120, 1), last)
    for a in range(4):
        last = pltpu.roll(edge_y, 7 - a, 1)
        block[5 * a + 4] = jnp.where(cell_y < 7, pltpu.roll(block[5 * a], 127, 1), last)
    last = jnp.where(cell_y < 7, pltpu.roll(block[20], 127, 1), pltpu.roll(edge_x, 24, 1))
    block[24] = jnp.where(cell_x < 7, pltpu.roll(block[4], 120, 1), last)
    joined = (row == 0) & (cell_z == 1)
    for k in range(25):
        other = pltpu.roll(pltpu.roll(block[k], 64, 1), 4, 0)
        block[k] = jnp.where(joined, other, block[k])
    return jnp.concatenate(block, axis=0)


def cell_order():
    rank, lane = row_iota((128, 128)), lane_iota((128, 128))
    x = (rank & 1) + 2 * (rank >> 3 & 1) + 4 * (rank >> 5 & 1)
    y = (rank >> 1 & 1) + 2 * (rank >> 4 & 1) + 4 * (rank >> 6 & 1)
    return jnp.where(64 * (rank >> 2 & 1) + 8 * x + y == lane, 1.0, 0.0)


def row_spread():
    row, node = row_iota((ROWS, 125)), lane_iota((ROWS, 125))
    return jnp.where(((row & 7) < 5) & (5 * (row >> 3) + (row & 7) == node), 1.0, 0.0)


def gather_kernel(
    live, wave_in, mass_in, conn_in, potential_in, levels_in, weights_in,
    nodal, face, inverse, cell_out,
    wave, mass, conn, potential, levels, weights, packed, low, high, stage, load_sem,
):
    loads = []
    sources = (conn_in, wave_in, mass_in, potential_in, levels_in, weights_in)
    targets = (conn, wave, mass, potential, levels, weights)
    for k in range(6):
        loads.append(pltpu.make_async_copy(sources[k], targets[k], load_sem.at[k]))
        loads[k].start()
    chunks = wave.shape[1] // 256
    vectors = wave.shape[0]
    group = vectors + 8
    stage[...] = jnp.zeros_like(stage)
    order, spread = cell_order(), row_spread()
    order_low, spread_low = order.astype(jnp.bfloat16), spread.astype(jnp.bfloat16)
    f32, bf16 = jnp.float32, jnp.bfloat16
    loads[0].wait()
    slots = conn[...]
    for part, target, nothing in ((slots >> 8, high, 63), (slots & 255, low, 0)):
        part = part.astype(f32).astype(bf16)
        spaced = jnp.dot(spread_low, part, preferred_element_type=f32)
        ordered = jnp.dot(spaced.astype(bf16), order_low, preferred_element_type=f32)
        ordered = ordered.astype(jnp.int32)
        target[:ROWS, :] = ordered
        edge_x, edge_y = pack_edges(blocks_of(ordered), nothing)
        target[ROWS:ROWS + 8, :] = edge_x
        target[ROWS + 8:ROWS + 16, :] = edge_y
    loads[1].wait()
    loads[2].wait()
    for chunk in range(chunks):
        columns = slice(256 * chunk, 256 * chunk + 256)
        scale = mass[:, columns]
        packed[group * chunk:group * chunk + vectors, :] = wave[:, columns] * scale
        packed[group * chunk + vectors:group * chunk + group, :] = jnp.broadcast_to(scale, (8, 256))
    value = packed[...]
    value_high = value.astype(bf16)
    value_low = (value - value_high.astype(f32)).astype(bf16)
    both = jnp.concatenate([value_high, value_low], axis=1)
    lane = lane_iota((1, 128))
    pair_lane = lane_iota((1, 256))
    blocks = [5 * a + b for a in range(4) for b in range(4)] + [25, 26]
    found = jnp.zeros((80, 256), f32)
    chunk_of = lax.broadcasted_iota(jnp.int32, (chunks, group, 256), 0)
    for i in range(GATHERED // 2):
        row = 8 * blocks[i // 2] + 1 + 2 * (i % 2)
        slot_low = jnp.concatenate([low[row:row + 1, :], low[row + 1:row + 2, :]], axis=1)
        slot_high = jnp.concatenate([high[row:row + 1, :], high[row + 1:row + 2, :]], axis=1)
        one_hot = jnp.where(row_iota((256, 256)) == slot_low, 1.0, 0.0).astype(bf16)
        twice = jnp.concatenate([one_hot, one_hot], axis=0)
        product = jnp.dot(both, twice, preferred_element_type=f32).reshape(chunks, group, 256)
        total = jnp.sum(jnp.where(chunk_of == slot_high[None], product, 0.0), axis=0)
        for part in range(2):
            start = (row + part) * group
            stage[start:start + group, :] = total[:, 128 * part:128 * part + 128]
        row_code = 2 * i + 1 + (pair_lane >> 7)
        cell_code = pair_lane & 127
        here = row_iota((40, 256)) == slot_high
        codes = jnp.concatenate(
            [jnp.where(here, row_code, 0), jnp.where(here, cell_code, 0)], axis=0
        ).astype(f32).astype(bf16)
        found = found + lax.dot_general(
            codes, one_hot, (((1,), (1,)), ((), ())), preferred_element_type=f32
        )
    inverse[...] = found
    tops = []
    for v in range(vectors + 1):
        column = fill_copies(blocks_of(stage[pl.ds(v, ROWS + 16, stride=group), :]))
        nodal[ROWS * v:ROWS * v + ROWS, :] = column
        tops.append(nodal[pl.ds(ROWS * v + 4, 25, stride=8), :])
    blank = jnp.zeros((7, 128), f32)
    for i in range(vectors // 2):
        pair = jnp.where(lane < 64, pltpu.roll(tops[2 * i], 64, 1), tops[2 * i + 1])
        face[i] = jnp.concatenate([pair, blank], axis=0).astype(bf16)
    top_high = tops[vectors].astype(bf16).astype(f32)
    parts = jnp.where(lane >= 64, tops[vectors] - top_high, pltpu.roll(top_high, 64, 1))
    face[vectors // 2] = jnp.concatenate([parts, blank], axis=0).astype(bf16)
    for k in range(3, 6):
        loads[k].wait()
    exact = lax.Precision.HIGHEST
    size = 1.0 / jnp.left_shift(1, levels[...]).astype(f32)
    in_use = jnp.where(lane < live[0], 1.0, 0.0)
    volume = size * size * size / 8.0 * in_use
    coefficient = volume * weights[:, 0:1] * potential[...]
    coefficient = jnp.dot(coefficient, order, precision=exact, preferred_element_type=f32)
    cell_out[:ROWS, :] = jnp.dot(spread, coefficient, precision=exact, preferred_element_type=f32)
    kinetic = jnp.broadcast_to(size / 4.0 * in_use, (8, 128))
    cell_out[ROWS:ROWS + 8, :] = jnp.dot(kinetic, order, precision=exact, preferred_element_type=f32)


def shared_sums(terms):
    lane = lane_iota((8, 128))
    row = row_iota((8, 128))
    cell_z, cell_x, cell_y = lane >> 6, lane >> 3 & 7, lane & 7
    block = [terms[8 * k:8 * k + 8] for k in range(25)]
    for b in range(5):
        first, last = block[b], block[20 + b]
        block[b] = first + jnp.where(cell_x > 0, pltpu.roll(last, 8, 1), 0.0)
        block[20 + b] = last + jnp.where(cell_x < 7, pltpu.roll(first, 120, 1), 0.0)
    for a in range(5):
        first, last = block[5 * a], block[5 * a + 4]
        block[5 * a] = first + jnp.where(cell_y > 0, pltpu.roll(last, 1, 1), 0.0)
        block[5 * a + 4] = last + jnp.where(cell_y < 7, pltpu.roll(first, 127, 1), 0.0)
    joined = ((row == 0) & (cell_z == 1)) | ((row == 4) & (cell_z == 0))
    for k in range(25):
        other = pltpu.roll(pltpu.roll(block[k], 64, 1), 4, 0)
        block[k] = block[k] + jnp.where(joined, other, 0.0)
    return jnp.concatenate(block, axis=0)


def cell_operator(pair, stiffness, cell_data):
    values = jnp.concatenate(pair, axis=1).astype(jnp.bfloat16)
    stiff = jnp.dot(stiffness, values, preferred_element_type=jnp.float32)
    coefficient, kinetic = cell_data[:ROWS], cell_data[ROWS:ROWS + 1]
    results = []
    for part in range(2):
        columns = slice(128 * part, 128 * part + 128)
        low = values[:, columns].astype(jnp.float32)
        results.append(shared_sums(kinetic * stiff[:, columns] + coefficient * low))
    return results


def mesh_id(peer, others):
    return (lax.div(peer, others), lax.rem(peer, others))


def meet_all(me, count, others):
    barrier = pltpu.get_barrier_semaphore()

    def greet(k, carry):
        peer = lax.rem(me + k, count)
        pl.semaphore_signal(
            barrier, inc=1, device_id=mesh_id(peer, others), device_id_type=pl.DeviceIdType.MESH
        )
        return carry

    lax.fori_loop(1, count, greet, 0)
    pl.semaphore_wait(barrier, count - 1)


def wait_bytes(ref, semaphore):
    pltpu.make_async_copy(ref, ref, semaphore).wait()


def filter_kernel(
    rows_of, others, bounds, nodal_in, face_in, inverse_in, cell_in, stiffness_in, wave_in, earlier,
    filtered, own_rows,
    nodal, inverse, cell_data, stiffness, wave, sums, degree, edge, spread_out, rounded,
    ghost, above, below, above_again, bottoms, tops, bottoms_again,
    held, quarter, partial, to_send, received, own_low, gathered, low_rows,
    input_sem, load_sem, ghost_send, ghost_recv, up_send, up_recv, down_send, down_recv,
    again_send, again_recv, swap_send, swap_recv, sum_send, sum_recv, all_send, all_recv,
):
    count = rows_of * others
    mine, along = lax.axis_index("vecs"), lax.axis_index("cells")
    me = along * others + mine
    vectors = wave.shape[0]
    pairs = vectors // 2
    width = earlier.shape[1]
    share = earlier.shape[0] // count
    half = share // 2
    parts = load_sem.shape[0]
    depth = earlier.shape[0] // parts
    blocks = depth // share
    first_part = lax.div(along * parts, rows_of) + 1
    columns = others * vectors
    f32, bf16 = jnp.float32, jnp.bfloat16
    center, halfwidth = bounds[0], bounds[1]
    lane = lane_iota((1, 128))
    inputs = []
    sources = (nodal_in, cell_in, stiffness_in, inverse_in, wave_in)
    targets = (nodal, cell_data, stiffness, inverse, wave)
    for k in range(5):
        inputs.append(pltpu.make_async_copy(sources[k], targets[k], input_sem.at[k]))
        inputs[k].start()
    has_above, has_below = along < rows_of - 1, along > 0

    def to_neighbour(source, target, step, send, recv):
        return pltpu.make_async_remote_copy(
            source, target, send, recv,
            device_id=(along + step, mine), device_id_type=pl.DeviceIdType.MESH,
        )

    meet_all(me, count, others)

    @pl.when(has_above)
    def _():
        to_neighbour(face_in, ghost, 1, ghost_send, ghost_recv).start()

    loads = []
    for k in range(parts):
        here = pl.ds(pl.multiple_of(lax.rem(first_part + k, parts) * depth, depth), depth)
        loads.append(pltpu.make_async_copy(earlier.at[here], held.at[here], load_sem.at[k]))
        loads[k].start()

    @pl.when(jnp.logical_not(has_above))
    def _():
        above[...] = jnp.zeros_like(above)
        above_again[...] = jnp.zeros_like(above_again)

    @pl.when(jnp.logical_not(has_below))
    def _():
        below[...] = jnp.zeros_like(below)
        ghost[...] = jnp.zeros_like(ghost)

    for k in range(5):
        inputs[k].wait()

    @pl.when(has_below)
    def _():
        wait_bytes(ghost, ghost_recv)

    for v in range(vectors + 1):
        got = ghost[v // 2].astype(f32)[:25]
        turned = pltpu.roll(got, 64, 1)
        value = got + turned if v == vectors else (turned if v % 2 else got)
        here = pl.ds(ROWS * v, 25, stride=8)
        nodal[here, :] = jnp.where(lane < 64, value, nodal[here, :])
    blank = jnp.zeros((7, 128), f32)

    def bottom_faces():
        first, second = edge[pl.ds(0, 25, stride=8), :], edge[pl.ds(ROWS, 25, stride=8), :]
        rows = jnp.where(lane < 64, first, pltpu.roll(second, 64, 1))
        return jnp.concatenate([rows, blank], axis=0).astype(bf16)

    def top_faces():
        first, second = edge[pl.ds(4, 25, stride=8), :], edge[pl.ds(ROWS + 4, 25, stride=8), :]
        rows = jnp.where(lane < 64, pltpu.roll(first, 64, 1), second)
        return jnp.concatenate([rows, blank], axis=0).astype(bf16)

    def add_above(faces):
        got = faces.astype(f32)[:25]
        for k, value in enumerate((pltpu.roll(got, 64, 1), got)):
            edge[pl.ds(ROWS * k + 4, 25, stride=8), :] += jnp.where(lane >= 64, value, 0.0)

    def add_below(faces):
        got = faces.astype(f32)[:25]
        for k, value in enumerate((got, pltpu.roll(got, 64, 1))):
            edge[pl.ds(ROWS * k, 25, stride=8), :] += jnp.where(lane < 64, value, 0.0)

    def both_rows(i):
        return pl.ds(pl.multiple_of(2 * ROWS * i, 16), 2 * ROWS)

    def apply(values):
        result = cell_operator(
            [values[:ROWS], values[ROWS:]], stiffness[:ROWS, :ROWS], cell_data[...]
        )
        for k in range(2):
            edge[ROWS * k:ROWS * k + ROWS, :] = result[k]

    def first_step(i, carry):
        apply(nodal[both_rows(i), :])
        sums[both_rows(i), :] = edge[...]
        bottoms[i] = bottom_faces()
        tops[i] = top_faces()

        @pl.when(has_below)
        def _():
            to_neighbour(bottoms.at[i], above.at[i], -1, up_send, up_recv.at[i]).start()

        @pl.when(has_above)
        def _():
            to_neighbour(tops.at[i], below.at[i], 1, down_send, down_recv.at[i]).start()

        return carry

    lax.fori_loop(0, pairs, first_step, 0)
    mass = nodal[ROWS * vectors:ROWS * vectors + ROWS, :]
    squared = jnp.concatenate([mass * mass, mass * mass], axis=0)

    def second_step(i, carry):
        @pl.when(has_above)
        def _():
            wait_bytes(above.at[i], up_recv.at[i])

        @pl.when(has_below)
        def _():
            wait_bytes(below.at[i], down_recv.at[i])

        edge[...] = sums[both_rows(i), :]
        add_above(above[i])
        add_below(below[i])
        one = (squared * edge[...] - center * nodal[both_rows(i), :]) / halfwidth
        degree[both_rows(i), :] = one
        apply(one)
        sums[both_rows(i), :] = edge[...]
        bottoms_again[i] = bottom_faces()

        @pl.when(has_below)
        def _():
            to_neighbour(
                bottoms_again.at[i], above_again.at[i], -1, again_send, again_recv.at[i]
            ).start()

        return carry

    lax.fori_loop(0, pairs, second_step, 0)
    unscale = 1.0 / jnp.where(mass == 0.0, 1.0, mass)
    for i in range(pairs):
        @pl.when(has_above)
        def _():
            wait_bytes(above_again.at[i], again_recv.at[i])

        here = both_rows(i)
        edge[...] = sums[here, :]
        add_above(above_again[i])
        two = 2.0 * (squared * edge[...] - center * degree[here, :]) / halfwidth - nodal[here, :]
        for k in range(2):
            v = 2 * i + k
            block = blocks_of(two[ROWS * k:ROWS * k + ROWS] * unscale)
            kept = [block[5 * a + b] for a in range(4) for b in range(4)]
            for n, part in enumerate(kept + list(pack_edges(block, 0.0))):
                spread_out[pl.ds(4 * n * vectors + v, 4, stride=vectors), :] = part[1:5]
    middle = GATHERED // 2 * vectors
    table = jnp.concatenate(
        [spread_out[:middle, :], spread_out[middle:2 * middle, :]], axis=1
    ).astype(bf16)
    chunks = width // 256
    row_of = lax.broadcasted_iota(jnp.int32, (GATHERED // 2, vectors, 256), 0)
    for q in range(others):
        peer = lax.rem(mine + 1 + q, others)
        for k in range(chunks):
            chunk = peer * chunks + k
            row_code = inverse[pl.ds(chunk, 1), :].astype(jnp.int32) - 1
            cell_code = inverse[pl.ds(40 + chunk, 1), :].astype(jnp.int32)
            second_half = row_code >= GATHERED // 2
            column = jnp.where(second_half, cell_code + 128, cell_code)
            row = jnp.where(second_half, row_code - GATHERED // 2, row_code)
            one_hot = jnp.where(row_iota((256, 256)) == column, 1.0, 0.0).astype(bf16)
            product = jnp.dot(table, one_hot, preferred_element_type=f32)
            product = product.reshape(GATHERED // 2, vectors, 256)
            total = jnp.sum(jnp.where(row_of == row[None], product, 0.0), axis=0)
            here = pl.ds(pl.multiple_of(chunk * 256, 256), 256)
            vector = wave[:, here]
            one = -center * vector / halfwidth
            unused = -2.0 * center * one / halfwidth - vector
            rounded[:, here] = jnp.where(row_code < 0, unused, total).astype(bf16)
        source = rounded.at[:, pl.ds(pl.multiple_of(peer * width, 128), width)]
        if q < others - 1:
            pltpu.make_async_remote_copy(
                source, quarter.at[mine], swap_send, swap_recv,
                device_id=(along, peer), device_id_type=pl.DeviceIdType.MESH,
            ).start()
        else:
            quarter[mine] = source[...]
    wait_bytes(quarter.at[pl.ds(0, others - 1)], swap_recv)
    vectors_here = quarter[...].reshape(columns, width)
    for k in range(parts):
        part = lax.rem(first_part + k, parts)
        loads[k].wait()
        result = lax.dot_general(
            held[pl.ds(pl.multiple_of(part * depth, depth), depth), :], vectors_here,
            (((1,), (1,)), ((), ())), preferred_element_type=jnp.float32,
        )
        for t in range(blocks):
            piece = result[share * t:share * t + share]
            piece = jnp.concatenate([piece[:half], piece[half:]], axis=1)
            partial[part * blocks + t] = piece
            to_send[part * blocks + t] = piece.astype(jnp.bfloat16)
        for t in range(blocks):
            owner = part * blocks + lax.rem(me + t, blocks)
            slot = lax.rem(owner - me + count, count) - 1

            @pl.when(owner != me)
            def _():
                pltpu.make_async_remote_copy(
                    to_send.at[owner], received.at[slot], sum_send, sum_recv,
                    device_id=mesh_id(owner, others), device_id_type=pl.DeviceIdType.MESH,
                ).start()

    wait_bytes(received, sum_recv)
    total = partial[me]
    for k in range(count - 1):
        total = total + received[k].astype(jnp.float32)
    own_rows[...] = jnp.concatenate([total[:, :columns], total[:, columns:]], axis=0)
    own_low[...] = total.astype(jnp.bfloat16)
    gathered[me] = own_low[...]
    for k in range(1, count):
        peer = lax.rem(me + k, count)
        pltpu.make_async_remote_copy(
            own_low, gathered.at[me], all_send, all_recv,
            device_id=mesh_id(peer, others), device_id_type=pl.DeviceIdType.MESH,
        ).start()
    wait_bytes(gathered.at[pl.ds(0, count - 1)], all_recv)
    for k in range(count):
        piece = gathered[k]
        low_rows[share * k:share * k + half, :] = piece[:, :columns]
        low_rows[share * k + half:share * k + share, :] = piece[:, columns:]
    weights = low_rows[...].astype(jnp.float32).T.astype(jnp.bfloat16)
    step = 256
    for start in range(0, width, step):
        here = slice(start, start + step)
        taken = jnp.dot(weights, held[:, here], preferred_element_type=jnp.float32)
        filtered[:, here] = vectors_here[:, here].astype(jnp.float32) - taken
    wait_bytes(quarter.at[pl.ds(0, others - 1)], swap_send)
    wait_bytes(received, sum_send)
    wait_bytes(gathered.at[pl.ds(0, count - 1)], all_send)

    @pl.when(has_above)
    def _():
        wait_bytes(ghost, ghost_send)
        wait_bytes(tops, down_send)

    @pl.when(has_below)
    def _():
        wait_bytes(bottoms, up_send)
        wait_bytes(bottoms_again, again_send)


def filter_block(bounds, nodal, face, inverse, cell_data, stiffness, wave_block, earlier_vectors):
    along, others = lax.axis_size("cells"), lax.axis_size("vecs")
    count = along * others
    vectors, owned = wave_block.shape
    depth, width = earlier_vectors.shape
    share, columns = depth // count, vectors * others
    bf16, f32 = jnp.bfloat16, jnp.float32
    dma = pltpu.SemaphoreType.DMA
    pairs = vectors // 2
    faces = pltpu.VMEM((pairs, 32, 128), bf16)
    block = (share // 2, 2 * columns)
    return pl.pallas_call(
        functools.partial(filter_kernel, along, others),
        out_shape=(
            jax.ShapeDtypeStruct((columns, width), f32),
            jax.ShapeDtypeStruct((share, columns), f32),
        ),
        in_specs=[pl.BlockSpec(memory_space=pltpu.SMEM)] + [pl.BlockSpec(memory_space=pl.ANY)] * 7,
        out_specs=(pl.BlockSpec(memory_space=pltpu.VMEM),) * 2,
        scratch_shapes=[
            pltpu.VMEM(nodal.shape, f32),
            pltpu.VMEM(inverse.shape, f32),
            pltpu.VMEM(cell_data.shape, f32),
            pltpu.VMEM(stiffness.shape, bf16),
            pltpu.VMEM((vectors, owned), f32),
            pltpu.VMEM((vectors * ROWS, 128), f32),
            pltpu.VMEM((vectors * ROWS, 128), f32),
            pltpu.VMEM((2 * ROWS, 128), f32),
            pltpu.VMEM((GATHERED * vectors, 128), f32),
            pltpu.VMEM((vectors, owned), bf16),
            pltpu.VMEM((pairs + 1, 32, 128), bf16),
            faces, faces, faces, faces, faces, faces,
            pltpu.VMEM((depth, width), bf16),
            pltpu.VMEM((others, vectors, width), bf16),
            pltpu.VMEM((count,) + block, f32),
            pltpu.VMEM((count,) + block, bf16),
            pltpu.VMEM((count - 1,) + block, bf16),
            pltpu.VMEM(block, bf16),
            pltpu.VMEM((count,) + block, bf16),
            pltpu.VMEM((depth, columns), bf16),
            dma((5,)), dma((4,)), dma, dma, dma, dma((pairs,)), dma, dma((pairs,)),
            dma, dma((pairs,)), dma, dma, dma, dma, dma, dma,
        ],
        compiler_params=pltpu.CompilerParams(
            collective_id=0, has_side_effects=True, vmem_limit_bytes=VMEM_BYTES
        ),
    )(bounds, nodal, face, inverse, cell_data, stiffness, wave_block, earlier_vectors)


def per_device(
    wave_block,
    connectivity,
    send_list,
    levels,
    live_cells,
    potential,
    mass_scale,
    center,
    halfwidth,
    earlier_vectors,
):
    stiffness, quadrature = fixed_tables()
    stiffness = jnp.asarray(stiffness).astype(jnp.bfloat16)
    weights = jnp.asarray(np.broadcast_to(quadrature[:, None], (125, 128)))
    vectors, owned = wave_block.shape
    nodes, cells = connectivity.shape
    group = vectors + 8
    f32, bf16 = jnp.float32, jnp.bfloat16
    shape = jax.ShapeDtypeStruct
    whole = pl.BlockSpec(memory_space=pltpu.VMEM)
    nodal, face, inverse, cell_data = pl.pallas_call(
        gather_kernel,
        out_shape=(
            shape(((vectors + 1) * ROWS, 128), f32),
            shape((vectors // 2 + 1, 32, 128), bf16),
            shape((80, 256), f32),
            shape((208, 128), f32),
        ),
        in_specs=[pl.BlockSpec(memory_space=pltpu.SMEM)] + [pl.BlockSpec(memory_space=pl.ANY)] * 6,
        out_specs=(whole,) * 4,
        scratch_shapes=[
            pltpu.VMEM((vectors, owned), f32),
            pltpu.VMEM((1, owned), f32),
            pltpu.VMEM((nodes, cells), jnp.int32),
            pltpu.VMEM((nodes, cells), f32),
            pltpu.VMEM((1, cells), jnp.int32),
            pltpu.VMEM((nodes, 128), f32),
            pltpu.VMEM((group * owned // 256, 256), f32),
            pltpu.VMEM((ROWS + 16, 128), jnp.int32),
            pltpu.VMEM((ROWS + 16, 128), jnp.int32),
            pltpu.VMEM(((ROWS + 16) * group, 128), f32),
            pltpu.SemaphoreType.DMA((6,)),
        ],
        compiler_params=pltpu.CompilerParams(vmem_limit_bytes=VMEM_BYTES),
    )(live_cells, wave_block, mass_scale[None], connectivity, potential, levels[None], weights)
    bounds = jnp.stack([center, halfwidth])
    share = earlier_vectors.shape[0] // lax.axis_size(("cells", "vecs"))
    return filter_block(
        bounds, nodal, face, inverse, cell_data, stiffness, wave_block, earlier_vectors
    )


def solution(mesh):
    in_specs = (
        P("vecs", "cells"),
        P(None, "cells"),
        P("cells"),
        P("cells"),
        P("cells"),
        P(None, "cells"),
        P("cells"),
        P(),
        P(),
        P(None, ("cells", "vecs")),
    )
    out_specs = (P(None, ("cells", "vecs")), P(("cells", "vecs"), None))
    return jax.shard_map(
        per_device, mesh=mesh, in_specs=in_specs, out_specs=out_specs, check_vma=False
    )
```

```python
import functools
import math

import jax
import jax.numpy as jnp
import numpy as np
from jax import lax
from jax.experimental import pallas as pl
from jax.experimental.pallas import tpu as pltpu
from jax.sharding import PartitionSpec as P

ROWS = 200
GATHERED = 72
VMEM_BYTES = 60 * 1024 * 1024


def gll_tables():
    root_value = math.sqrt(3.0 / 7.0)
    points = np.array([-1.0, -root_value, 0.0, root_value, 1.0])
    weights = np.array([0.1, 49.0 / 90.0, 32.0 / 45.0, 49.0 / 90.0, 0.1])
    barycentric = np.ones(5)
    for node_index in range(5):
        for other_node in range(5):
            if other_node != node_index:
                barycentric[node_index] = barycentric[node_index] / (
                    points[node_index] - points[other_node]
                )
    derivative = np.zeros((5, 5))
    for row_index in range(5):
        for col_index in range(5):
            if row_index != col_index:
                derivative[row_index, col_index] = (
                    barycentric[col_index]
                    / barycentric[row_index]
                    / (points[row_index] - points[col_index])
                )
        derivative[row_index, row_index] = -np.sum(derivative[row_index])
    mass_one = np.zeros((5, 5))
    for node_index in range(5):
        mass_one[node_index, node_index] = weights[node_index]
    laplace_one = derivative.T @ mass_one @ derivative
    stiffness = (
        np.kron(np.kron(laplace_one, mass_one), mass_one)
        + np.kron(np.kron(mass_one, laplace_one), mass_one)
        + np.kron(np.kron(mass_one, mass_one), laplace_one)
    )
    quadrature = np.kron(np.kron(weights, weights), weights)
    return (stiffness.astype(np.float32), quadrature.astype(np.float32))


def fixed_tables():
    stiffness, quadrature = gll_tables()
    spread = np.zeros((ROWS, 125), np.float32)
    for j in range(125):
        spread[8 * (j // 5) + j % 5, j] = 1.0
    padded = np.zeros((208, 256), np.float32)
    padded[:ROWS, :ROWS] = spread @ stiffness @ spread.T
    return padded, quadrature


def lane_iota(shape):
    return lax.broadcasted_iota(jnp.int32, shape, 1)


def row_iota(shape):
    return lax.broadcasted_iota(jnp.int32, shape, 0)


def blocks_of(value):
    return [value[8 * k:8 * k + 8] for k in range(value.shape[0] // 8)]


def pack_edges(block, nothing):
    lane = lane_iota((8, 128))
    cell_x, cell_y = lane >> 3 & 7, lane & 7
    edge_x = jnp.full((8, 128), nothing, block[0].dtype)
    edge_y = edge_x
    for b in range(4):
        edge_x = jnp.where(cell_x == b, pltpu.roll(block[20 + b], 128 - 8 * (7 - b), 1), edge_x)
    corner = (cell_x == 4) & (cell_y == 7)
    edge_x = jnp.where(corner, pltpu.roll(block[24], 128 - 24, 1), edge_x)
    for a in range(4):
        edge_y = jnp.where(cell_y == a, pltpu.roll(block[5 * a + 4], 128 - (7 - a), 1), edge_y)
    return edge_x, edge_y


def fill_copies(block):
    lane = lane_iota((8, 128))
    row = row_iota((8, 128))
    cell_z, cell_x, cell_y = lane >> 6, lane >> 3 & 7, lane & 7
    edge_x, edge_y = block[25], block[26]
    block = block[:25]
    for b in range(4):
        last = pltpu.roll(edge_x, 8 * (7 - b), 1) if b < 7 else edge_x
        block[20 + b] = jnp.where(cell_x < 7, pltpu.roll(block[b], 120, 1), last)
    for a in range(4):
        last = pltpu.roll(edge_y, 7 - a, 1)
        block[5 * a + 4] = jnp.where(cell_y < 7, pltpu.roll(block[5 * a], 127, 1), last)
    last = jnp.where(cell_y < 7, pltpu.roll(block[20], 127, 1), pltpu.roll(edge_x, 24, 1))
    block[24] = jnp.where(cell_x < 7, pltpu.roll(block[4], 120, 1), last)
    joined = (row == 0) & (cell_z == 1)
    for k in range(25):
        other = pltpu.roll(pltpu.roll(block[k], 64, 1), 4, 0)
        block[k] = jnp.where(joined, other, block[k])
    return jnp.concatenate(block, axis=0)


def cell_order():
    rank, lane = row_iota((128, 128)), lane_iota((128, 128))
    x = (rank & 1) + 2 * (rank >> 3 & 1) + 4 * (rank >> 5 & 1)
    y = (rank >> 1 & 1) + 2 * (rank >> 4 & 1) + 4 * (rank >> 6 & 1)
    return jnp.where(64 * (rank >> 2 & 1) + 8 * x + y == lane, 1.0, 0.0)


def row_spread():
    row, node = row_iota((ROWS, 125)), lane_iota((ROWS, 125))
    return jnp.where(((row & 7) < 5) & (5 * (row >> 3) + (row & 7) == node), 1.0, 0.0)


def node_weights():
    node = row_iota((125, 128))

    def weight(index):
        return jnp.where(index == 2, 32.0 / 45.0, jnp.where((index & 3) == 0, 0.1, 49.0 / 90.0))

    a, ab = node * 41 >> 10, node * 205 >> 10
    return weight(a) * weight(ab - 5 * a) * weight(node - 5 * ab)


def gather_nodes(
    live, wave, mass, conn, potential, levels, nodal, face, inverse, cell_out,
    packed, low, high, stage, loads,
):
    chunks = wave.shape[1] // 256
    vectors = wave.shape[0]
    group = vectors + 8
    stage[...] = jnp.zeros_like(stage)
    order, spread = cell_order(), row_spread()
    order_low, spread_low = order.astype(jnp.bfloat16), spread.astype(jnp.bfloat16)
    f32, bf16 = jnp.float32, jnp.bfloat16
    loads[0].wait()
    slots = conn[...]
    for part, target, nothing in ((slots >> 8, high, 63), (slots & 255, low, 0)):
        part = part.astype(f32).astype(bf16)
        spaced = jnp.dot(spread_low, part, preferred_element_type=f32)
        ordered = jnp.dot(spaced.astype(bf16), order_low, preferred_element_type=f32)
        ordered = ordered.astype(jnp.int32)
        target[:ROWS, :] = ordered
        edge_x, edge_y = pack_edges(blocks_of(ordered), nothing)
        target[ROWS:ROWS + 8, :] = edge_x
        target[ROWS + 8:ROWS + 16, :] = edge_y
    loads[1].wait()
    loads[2].wait()
    for chunk in range(chunks):
        columns = slice(256 * chunk, 256 * chunk + 256)
        scale = mass[:, columns]
        packed[group * chunk:group * chunk + vectors, :] = wave[:, columns] * scale
        packed[group * chunk + vectors:group * chunk + group, :] = jnp.broadcast_to(scale, (8, 256))
    value = packed[...]
    value_high = value.astype(bf16)
    value_low = (value - value_high.astype(f32)).astype(bf16)
    both = jnp.concatenate([value_high, value_low], axis=1)
    lane = lane_iota((1, 128))
    pair_lane = lane_iota((1, 256))
    blocks = [5 * a + b for a in range(4) for b in range(4)] + [25, 26]
    found = jnp.zeros((80, 256), f32)
    chunk_of = lax.broadcasted_iota(jnp.int32, (chunks, group, 256), 0)
    for i in range(GATHERED // 2):
        row = 8 * blocks[i // 2] + 1 + 2 * (i % 2)
        slot_low = jnp.concatenate([low[row:row + 1, :], low[row + 1:row + 2, :]], axis=1)
        slot_high = jnp.concatenate([high[row:row + 1, :], high[row + 1:row + 2, :]], axis=1)
        one_hot = jnp.where(row_iota((256, 256)) == slot_low, 1.0, 0.0).astype(bf16)
        twice = jnp.concatenate([one_hot, one_hot], axis=0)
        product = jnp.dot(both, twice, preferred_element_type=f32).reshape(chunks, group, 256)
        total = jnp.sum(jnp.where(chunk_of == slot_high[None], product, 0.0), axis=0)
        for part in range(2):
            start = (row + part) * group
            stage[start:start + group, :] = total[:, 128 * part:128 * part + 128]
        row_code = 2 * i + 1 + (pair_lane >> 7)
        cell_code = pair_lane & 127
        here = row_iota((40, 256)) == slot_high
        codes = jnp.concatenate(
            [jnp.where(here, row_code, 0), jnp.where(here, cell_code, 0)], axis=0
        ).astype(f32).astype(bf16)
        found = found + lax.dot_general(
            codes, one_hot, (((1,), (1,)), ((), ())), preferred_element_type=f32
        )
    inverse[...] = found
    tops = []
    for v in range(vectors + 1):
        column = fill_copies(blocks_of(stage[pl.ds(v, ROWS + 16, stride=group), :]))
        nodal[ROWS * v:ROWS * v + ROWS, :] = column
        tops.append(nodal[pl.ds(ROWS * v + 4, 25, stride=8), :])
    blank = jnp.zeros((7, 128), f32)
    for i in range(vectors // 2):
        pair = jnp.where(lane < 64, pltpu.roll(tops[2 * i], 64, 1), tops[2 * i + 1])
        face[i] = jnp.concatenate([pair, blank], axis=0).astype(bf16)
    top_high = tops[vectors].astype(bf16).astype(f32)
    parts = jnp.where(lane >= 64, tops[vectors] - top_high, pltpu.roll(top_high, 64, 1))
    face[vectors // 2] = jnp.concatenate([parts, blank], axis=0).astype(bf16)
    loads[3].wait()
    loads[4].wait()
    exact = lax.Precision.HIGHEST
    size = 1.0 / jnp.left_shift(1, levels[...]).astype(f32)
    in_use = jnp.where(lane < live[0], 1.0, 0.0)
    volume = size * size * size / 8.0 * in_use
    coefficient = volume * node_weights() * potential[...]
    coefficient = jnp.dot(coefficient, order, precision=exact, preferred_element_type=f32)
    cell_out[:ROWS, :] = jnp.dot(spread, coefficient, precision=exact, preferred_element_type=f32)
    kinetic = jnp.broadcast_to(size / 4.0 * in_use, (8, 128))
    cell_out[ROWS:ROWS + 8, :] = jnp.dot(kinetic, order, precision=exact, preferred_element_type=f32)


def shared_sums(terms):
    lane = lane_iota((8, 128))
    row = row_iota((8, 128))
    cell_z, cell_x, cell_y = lane >> 6, lane >> 3 & 7, lane & 7
    block = [terms[8 * k:8 * k + 8] for k in range(25)]
    for b in range(5):
        first, last = block[b], block[20 + b]
        block[b] = first + jnp.where(cell_x > 0, pltpu.roll(last, 8, 1), 0.0)
        block[20 + b] = last + jnp.where(cell_x < 7, pltpu.roll(first, 120, 1), 0.0)
    for a in range(5):
        first, last = block[5 * a], block[5 * a + 4]
        block[5 * a] = first + jnp.where(cell_y > 0, pltpu.roll(last, 1, 1), 0.0)
        block[5 * a + 4] = last + jnp.where(cell_y < 7, pltpu.roll(first, 127, 1), 0.0)
    joined = ((row == 0) & (cell_z == 1)) | ((row == 4) & (cell_z == 0))
    for k in range(25):
        other = pltpu.roll(pltpu.roll(block[k], 64, 1), 4, 0)
        block[k] = block[k] + jnp.where(joined, other, 0.0)
    return jnp.concatenate(block, axis=0)


def cell_operator(pair, stiffness, cell_data):
    values = jnp.concatenate(pair, axis=1).astype(jnp.bfloat16)
    stiff = jnp.dot(stiffness, values, preferred_element_type=jnp.float32)
    coefficient, kinetic = cell_data[:ROWS], cell_data[ROWS:ROWS + 1]
    results = []
    for part in range(len(pair)):
        columns = slice(128 * part, 128 * part + 128)
        low = values[:, columns].astype(jnp.float32)
        results.append(shared_sums(kinetic * stiff[:, columns] + coefficient * low))
    return results


def mesh_id(peer, others):
    return (lax.div(peer, others), lax.rem(peer, others))


def greet_all(me, count, others):
    barrier = pltpu.get_barrier_semaphore()

    def greet(k, carry):
        peer = lax.rem(me + k, count)
        pl.semaphore_signal(
            barrier, inc=1, device_id=mesh_id(peer, others), device_id_type=pl.DeviceIdType.MESH
        )
        return carry

    lax.fori_loop(1, count, greet, 0)
    return barrier


def wait_bytes(ref, semaphore):
    pltpu.make_async_copy(ref, ref, semaphore).wait()


def filter_kernel(
    rows_of, others, bounds, live,
    wave_in, mass_in, conn_in, potential_in, levels_in, stiffness_in, earlier,
    filtered, own_rows,
    wave, mass_row, conn, potential, levels, stiffness, packed, low, high, stage,
    nodal, face, inverse, cell_data, sums, degree, spread_out, rounded,
    ghost, above, below, above_again, bottoms, tops, bottoms_again,
    held, quarter, partial, to_send, received, own_low, gathered, low_rows,
    input_sem, load_sem, ghost_send, ghost_recv, up_send, up_recv, down_send, down_recv,
    again_send, again_recv, swap_send, swap_recv, sum_send, sum_recv, all_send, all_recv,
):
    count = rows_of * others
    mine, along = lax.axis_index("vecs"), lax.axis_index("cells")
    me = along * others + mine
    vectors = wave.shape[0]
    pairs = vectors // 2
    width = earlier.shape[1]
    share = earlier.shape[0] // count
    half = share // 2
    parts = load_sem.shape[0]
    depth = earlier.shape[0] // parts
    blocks = depth // share
    first_part = lax.div(along * parts, rows_of) + 1
    columns = others * vectors
    f32, bf16 = jnp.float32, jnp.bfloat16
    center, halfwidth = bounds[0], bounds[1]
    lane = lane_iota((1, 128))
    inputs = []
    sources = (conn_in, wave_in, mass_in, potential_in, levels_in, stiffness_in)
    targets = (conn, wave, mass_row, potential, levels, stiffness)
    for k in range(6):
        inputs.append(pltpu.make_async_copy(sources[k], targets[k], input_sem.at[k]))
        inputs[k].start()
    loads = []
    for k in range(parts):
        here = pl.ds(pl.multiple_of(lax.rem(first_part + k, parts) * depth, depth), depth)
        loads.append(pltpu.make_async_copy(earlier.at[here], held.at[here], load_sem.at[k]))
        loads[k].start()
    barrier = greet_all(me, count, others)
    has_above, has_below = along < rows_of - 1, along > 0

    def to_neighbour(source, target, step, send, recv):
        return pltpu.make_async_remote_copy(
            source, target, send, recv,
            device_id=(along + step, mine), device_id_type=pl.DeviceIdType.MESH,
        )

    gather_nodes(
        live, wave, mass_row, conn, potential, levels, nodal, face, inverse, cell_data,
        packed, low, high, stage, inputs,
    )
    pl.semaphore_wait(barrier, count - 1)

    @pl.when(has_above)
    def _():
        to_neighbour(face, ghost, 1, ghost_send, ghost_recv).start()

    @pl.when(jnp.logical_not(has_above))
    def _():
        above[...] = jnp.zeros_like(above)
        above_again[...] = jnp.zeros_like(above_again)

    @pl.when(jnp.logical_not(has_below))
    def _():
        below[...] = jnp.zeros_like(below)
        ghost[...] = jnp.zeros_like(ghost)

    inputs[5].wait()

    @pl.when(has_below)
    def _():
        wait_bytes(ghost, ghost_recv)

    for v in range(vectors + 1):
        got = ghost[v // 2].astype(f32)[:25]
        turned = pltpu.roll(got, 64, 1)
        value = got + turned if v == vectors else (turned if v % 2 else got)
        here = pl.ds(ROWS * v, 25, stride=8)
        nodal[here, :] = jnp.where(lane < 64, value, nodal[here, :])
    blank = jnp.zeros((7, 128), f32)

    def rows(v, first, size, stride):
        return pl.ds(ROWS * v + first, size, stride=stride)

    def bottom_faces(i):
        first, second = sums[rows(2 * i, 0, 25, 8), :], sums[rows(2 * i + 1, 0, 25, 8), :]
        joined = jnp.where(lane < 64, first, pltpu.roll(second, 64, 1))
        return jnp.concatenate([joined, blank], axis=0).astype(bf16)

    def top_faces(i):
        first, second = sums[rows(2 * i, 4, 25, 8), :], sums[rows(2 * i + 1, 4, 25, 8), :]
        joined = jnp.where(lane < 64, pltpu.roll(first, 64, 1), second)
        return jnp.concatenate([joined, blank], axis=0).astype(bf16)

    def add_above(i, faces):
        got = faces.astype(f32)[:25]
        for k, value in enumerate((pltpu.roll(got, 64, 1), got)):
            sums[rows(2 * i + k, 4, 25, 8), :] += jnp.where(lane >= 64, value, 0.0)

    def add_below(i, faces):
        got = faces.astype(f32)[:25]
        for k, value in enumerate((got, pltpu.roll(got, 64, 1))):
            sums[rows(2 * i + k, 0, 25, 8), :] += jnp.where(lane < 64, value, 0.0)

    steps = pairs // 2

    def vector(v):
        return slice(ROWS * v, ROWS * v + ROWS)

    def apply(g, values):
        result = cell_operator(values, stiffness[:ROWS, :ROWS], cell_data[...])
        for k in range(4):
            sums[vector(4 * g + k), :] = result[k]

    for g in range(steps):
        both = pl.ds(2 * g, 2)
        apply(g, [nodal[vector(4 * g + k), :] for k in range(4)])
        for i in (2 * g, 2 * g + 1):
            bottoms[i] = bottom_faces(i)
            tops[i] = top_faces(i)

        @pl.when(has_below)
        def _():
            to_neighbour(bottoms.at[both], above.at[both], -1, up_send, up_recv.at[g]).start()

        @pl.when(has_above)
        def _():
            to_neighbour(tops.at[both], below.at[both], 1, down_send, down_recv.at[g]).start()

    mass = nodal[ROWS * vectors:ROWS * vectors + ROWS, :]
    squared = mass * mass
    for g in range(steps):
        both = pl.ds(2 * g, 2)

        @pl.when(has_above)
        def _():
            wait_bytes(above.at[both], up_recv.at[g])

        @pl.when(has_below)
        def _():
            wait_bytes(below.at[both], down_recv.at[g])

        for i in (2 * g, 2 * g + 1):
            add_above(i, above[i])
            add_below(i, below[i])
        ones = []
        for v in range(4 * g, 4 * g + 4):
            ones.append((squared * sums[vector(v), :] - center * nodal[vector(v), :]) / halfwidth)
            degree[vector(v), :] = ones[-1]
        apply(g, ones)
        for i in (2 * g, 2 * g + 1):
            bottoms_again[i] = bottom_faces(i)

        @pl.when(has_below)
        def _():
            to_neighbour(
                bottoms_again.at[both], above_again.at[both], -1, again_send, again_recv.at[g]
            ).start()

    unscale = 1.0 / jnp.where(mass == 0.0, 1.0, mass)
    for g in range(steps):
        @pl.when(has_above)
        def _():
            wait_bytes(above_again.at[pl.ds(2 * g, 2)], again_recv.at[g])

        for i in (2 * g, 2 * g + 1):
            add_above(i, above_again[i])
        for v in range(4 * g, 4 * g + 4):
            one = degree[vector(v), :]
            two = 2.0 * (squared * sums[vector(v), :] - center * one) / halfwidth
            block = blocks_of((two - nodal[vector(v), :]) * unscale)
            kept = [block[5 * a + b] for a in range(4) for b in range(4)]
            for n, part in enumerate(kept + list(pack_edges(block, 0.0))):
                spread_out[pl.ds(4 * n * vectors + v, 4, stride=vectors), :] = part[1:5]
    middle = GATHERED // 2 * vectors
    table = jnp.concatenate(
        [spread_out[:middle, :], spread_out[middle:2 * middle, :]], axis=1
    ).astype(bf16)
    chunks = width // 256
    row_of = lax.broadcasted_iota(jnp.int32, (GATHERED // 2, vectors, 256), 0)
    for q in range(others):
        peer = lax.rem(mine + 1 + q, others)
        for k in range(chunks):
            chunk = peer * chunks + k
            row_code = inverse[pl.ds(chunk, 1), :].astype(jnp.int32) - 1
            cell_code = inverse[pl.ds(40 + chunk, 1), :].astype(jnp.int32)
            second_half = row_code >= GATHERED // 2
            column = jnp.where(second_half, cell_code + 128, cell_code)
            row = jnp.where(second_half, row_code - GATHERED // 2, row_code)
            one_hot = jnp.where(row_iota((256, 256)) == column, 1.0, 0.0).astype(bf16)
            product = jnp.dot(table, one_hot, preferred_element_type=f32)
            product = product.reshape(GATHERED // 2, vectors, 256)
            total = jnp.sum(jnp.where(row_of == row[None], product, 0.0), axis=0)
            here = pl.ds(pl.multiple_of(chunk * 256, 256), 256)
            wanted = wave[:, here]
            one = -center * wanted / halfwidth
            unused = -2.0 * center * one / halfwidth - wanted
            rounded[:, here] = jnp.where(row_code < 0, unused, total).astype(bf16)
        source = rounded.at[:, pl.ds(pl.multiple_of(peer * width, 128), width)]
        if q < others - 1:
            pltpu.make_async_remote_copy(
                source, quarter.at[mine], swap_send, swap_recv,
                device_id=(along, peer), device_id_type=pl.DeviceIdType.MESH,
            ).start()
        else:
            quarter[mine] = source[...]
    wait_bytes(quarter.at[pl.ds(0, others - 1)], swap_recv)
    vectors_here = quarter[...].reshape(columns, width)
    for k in range(parts):
        part = lax.rem(first_part + k, parts)
        loads[k].wait()
        result = lax.dot_general(
            held[pl.ds(pl.multiple_of(part * depth, depth), depth), :], vectors_here,
            (((1,), (1,)), ((), ())), preferred_element_type=jnp.float32,
        )
        for t in range(blocks):
            piece = result[share * t:share * t + share]
            piece = jnp.concatenate([piece[:half], piece[half:]], axis=1)
            partial[part * blocks + t] = piece
            to_send[part * blocks + t] = piece.astype(jnp.bfloat16)
        for t in range(blocks):
            owner = part * blocks + lax.rem(me + t, blocks)
            slot = lax.rem(owner - me + count, count) - 1

            @pl.when(owner != me)
            def _():
                pltpu.make_async_remote_copy(
                    to_send.at[owner], received.at[slot], sum_send, sum_recv,
                    device_id=mesh_id(owner, others), device_id_type=pl.DeviceIdType.MESH,
                ).start()

    wait_bytes(received, sum_recv)
    total = partial[me]
    for k in range(count - 1):
        total = total + received[k].astype(jnp.float32)
    own_rows[...] = jnp.concatenate([total[:, :columns], total[:, columns:]], axis=0)
    own_low[...] = total.astype(jnp.bfloat16)
    gathered[me] = own_low[...]
    own_part = lax.div(me, blocks)
    for k in range(1, count):
        peer = lax.rem(me + k, count)
        pltpu.make_async_remote_copy(
            own_low, gathered.at[me], all_send, all_recv.at[own_part],
            device_id=mesh_id(peer, others), device_id_type=pl.DeviceIdType.MESH,
        ).start()
    for k in range(parts):
        part = lax.rem(own_part + k, parts)
        come = blocks - 1 if k == 0 else blocks
        wait_bytes(gathered.at[pl.ds(0, come)], all_recv.at[part])
        for t in range(blocks):
            piece = gathered[part * blocks + t]
            low_rows[share * t:share * t + half, :] = piece[:, :columns]
            low_rows[share * t + half:share * t + share, :] = piece[:, columns:]
        weights = low_rows[...].astype(jnp.float32).T.astype(jnp.bfloat16)
        deep = pl.ds(pl.multiple_of(part * depth, depth), depth)
        for start in range(0, width, 256):
            here = slice(start, start + 256)
            taken = jnp.dot(weights, held[deep, here], preferred_element_type=jnp.float32)
            base = vectors_here[:, here].astype(jnp.float32) if k == 0 else filtered[:, here]
            filtered[:, here] = base - taken
    wait_bytes(quarter.at[pl.ds(0, others - 1)], swap_send)
    wait_bytes(received, sum_send)
    wait_bytes(gathered.at[pl.ds(0, count - 1)], all_send)

    @pl.when(has_above)
    def _():
        wait_bytes(ghost, ghost_send)
        wait_bytes(tops, down_send)

    @pl.when(has_below)
    def _():
        wait_bytes(bottoms, up_send)
        wait_bytes(bottoms_again, again_send)


def per_device(
    wave_block,
    connectivity,
    send_list,
    levels,
    live_cells,
    potential,
    mass_scale,
    center,
    halfwidth,
    earlier_vectors,
):
    stiffness, _ = fixed_tables()
    stiffness = jnp.asarray(stiffness).astype(jnp.bfloat16)
    along, others = lax.axis_size("cells"), lax.axis_size("vecs")
    count = along * others
    vectors, owned = wave_block.shape
    nodes, cells = connectivity.shape
    depth, width = earlier_vectors.shape
    share, columns = depth // count, vectors * others
    group, pairs = vectors + 8, vectors // 2
    parts, steps = 4, vectors // 4
    bf16, f32 = jnp.bfloat16, jnp.float32
    dma = pltpu.SemaphoreType.DMA
    faces = pltpu.VMEM((pairs, 32, 128), bf16)
    all_faces = pltpu.VMEM((pairs + 1, 32, 128), bf16)
    block = (share // 2, 2 * columns)
    return pl.pallas_call(
        functools.partial(filter_kernel, along, others),
        out_shape=(
            jax.ShapeDtypeStruct((columns, width), f32),
            jax.ShapeDtypeStruct((share, columns), f32),
        ),
        in_specs=[pl.BlockSpec(memory_space=pltpu.SMEM)] * 2
        + [pl.BlockSpec(memory_space=pl.ANY)] * 7,
        out_specs=(pl.BlockSpec(memory_space=pltpu.VMEM),) * 2,
        scratch_shapes=[
            pltpu.VMEM((vectors, owned), f32),
            pltpu.VMEM((1, owned), f32),
            pltpu.VMEM((nodes, cells), jnp.int32),
            pltpu.VMEM((nodes, cells), f32),
            pltpu.VMEM((1, cells), jnp.int32),
            pltpu.VMEM(stiffness.shape, bf16),
            pltpu.VMEM((group * owned // 256, 256), f32),
            pltpu.VMEM((ROWS + 16, 128), jnp.int32),
            pltpu.VMEM((ROWS + 16, 128), jnp.int32),
            pltpu.VMEM(((ROWS + 16) * group, 128), f32),
            pltpu.VMEM(((vectors + 1) * ROWS, 128), f32),
            all_faces,
            pltpu.VMEM((80, 256), f32),
            pltpu.VMEM((ROWS + 8, 128), f32),
            pltpu.VMEM((vectors * ROWS, 128), f32),
            pltpu.VMEM((vectors * ROWS, 128), f32),
            pltpu.VMEM((GATHERED * vectors, 128), f32),
            pltpu.VMEM((vectors, owned), bf16),
            all_faces,
            faces, faces, faces, faces, faces, faces,
            pltpu.VMEM((depth, width), bf16),
            pltpu.VMEM((others, vectors, width), bf16),
            pltpu.VMEM((count,) + block, f32),
            pltpu.VMEM((count,) + block, bf16),
            pltpu.VMEM((count - 1,) + block, bf16),
            pltpu.VMEM(block, bf16),
            pltpu.VMEM((count,) + block, bf16),
            pltpu.VMEM((depth // parts, columns), bf16),
            dma((6,)), dma((parts,)), dma, dma, dma, dma((steps,)), dma, dma((steps,)),
            dma, dma((steps,)), dma, dma, dma, dma, dma, dma((parts,)),
        ],
        compiler_params=pltpu.CompilerParams(
            collective_id=0, has_side_effects=True, vmem_limit_bytes=VMEM_BYTES
        ),
    )(
        jnp.stack([center, halfwidth]), live_cells, wave_block, mass_scale[None], connectivity,
        potential, levels[None], stiffness, earlier_vectors,
    )


def solution(mesh):
    in_specs = (
        P("vecs", "cells"),
        P(None, "cells"),
        P("cells"),
        P("cells"),
        P("cells"),
        P(None, "cells"),
        P("cells"),
        P(),
        P(),
        P(None, ("cells", "vecs")),
    )
    out_specs = (P(None, ("cells", "vecs")), P(("cells", "vecs"), None))
    return jax.shard_map(
        per_device, mesh=mesh, in_specs=in_specs, out_specs=out_specs, check_vma=False
    )
```
